128 devices in a mesh: seq: 32 (over x, z, core), head: 4 (over y).
Axes of the slice: x: 4, y: 4, z: 4, core: 2. Of those that a mesh axis runs over, the one named last changes fastest.
Arguments:
- tokens: bfloat16 [16384, 4096], P('seq', 'head'), may hold values from -80 to 80, as said below
- w_query: bfloat16 [4096, 2048], P(None, 'head'), may hold values from -0.09375 to 0.09375
- w_key: bfloat16 [4096, 2048], P(None, 'head'), may hold values from -0.09375 to 0.09375
- w_value: bfloat16 [4096, 2048], P(None, 'head'), may hold values from -0.09375 to 0.09375
- w_out: bfloat16 [2048, 4096], P('head'), may hold values from -0.125 to 0.125
- block_bucket: int32 [128], P('seq'), may hold values from 0 to 575, as said below
Outputs:
- attended: bfloat16 [16384, 4096], P('seq', 'head')
The draws below stay inside these ranges and needn't reach their ends.
Inputs may be any that keep to these rules, and one draw needn't show every extreme that they name: `tokens`: hidden states of order one; a few rows may be far larger. `block_bucket`: no bucket holds more than 2 blocks, and some bucket holds exactly 2; an owner's buckets are numbered from its first id on and hold 2 blocks each except possibly its first and its last. The blocks of one index of seq belong to buckets of at most 1 block per owner, and some owner receives exactly 1 from every index of seq.
All inputs are finite; a program needn't handle non-finite values.
Results may differ from the reference program's by a relative error of at most 0.012.
The reference program's roundings to bfloat16 on the way (of `query`, `keys`, `values`, `weights` and `mixed`) count: a program that leaves them out, or rounds other values in their place, can miss the bound.
Values may be sent and summed in bfloat16 or wider, within the bound.
A program may use at most 128 MiB of HBM per device.

```python
import jax
import jax.numpy as jnp
from jax import lax

D = 4096
HEADS = 16
HDIM = 128
BLOCK = 128
BMAX = 2
BLK_DEV = 4
NBLK = 128
TOKENS = 16384
BUCK_OWN = 18
N_SEQ = 32


def draw_tokens(key, part):
    first = jax.random.fold_in(key, 0)
    base = jnp.clip(jax.random.normal(first, (TOKENS, D), jnp.float32), -5.0, 5.0)
    values = base
    return values.astype(jnp.bfloat16)


def draw_block_bucket(key, part):
    base = jax.random.fold_in(key, 11)
    first, second, third, fourth, fifth = jax.random.split(base, 5)
    picked = min(BLK_DEV, N_SEQ)
    hot_count = max(1, picked // 4)
    hot = (jax.random.permutation(first, N_SEQ) < hot_count).astype(jnp.int32)
    noise = jax.random.randint(second, (N_SEQ, N_SEQ), 0, 1 << 16)
    score = (noise + hot[None, :] * (1 << 17)) * N_SEQ + jnp.arange(N_SEQ, dtype=jnp.int32)[None, :]
    order = jnp.argsort(-score, axis=1).astype(jnp.int32)
    chosen = order[:, :picked]
    shuffle_keys = jax.random.randint(third, (N_SEQ, BLK_DEV), 0, 1 << 16) * BLK_DEV + jnp.arange(BLK_DEV, dtype=jnp.int32)[None, :]
    shuffled = jnp.argsort(shuffle_keys, axis=1).astype(jnp.int32)
    owner = jnp.take_along_axis(chosen, shuffled % picked, axis=1).reshape(NBLK)
    random_order = jax.random.randint(fourth, (NBLK,), 0, 1 << 16) * NBLK + jnp.arange(NBLK, dtype=jnp.int32)
    before = (owner[:, None] == owner[None, :]) & (random_order[None, :] < random_order[:, None])
    rank = jnp.sum(before.astype(jnp.int32), axis=1)
    shift = jax.random.randint(fifth, (N_SEQ,), 0, BMAX)
    local = (rank + jnp.take(shift, owner)) // BMAX
    return (owner * BUCK_OWN + local).astype(jnp.int32)


def shard_levels(own_key, extent, cuts, smallest, largest):
    gain = 1.0
    for dim, parts in cuts:
        draws = jax.random.uniform(jax.random.fold_in(jax.random.fold_in(own_key, 6), dim), (parts,), jnp.float32, smallest / len(cuts), largest / len(cuts))
        gain = gain * jnp.repeat(jnp.exp(draws), extent[dim] // parts).reshape((-1,) + (1,) * (len(extent) - 1 - dim))
    return gain


def centred(key, dims, spread, limit, pieces=(), kind=jnp.bfloat16):
    gain = shard_levels(key, dims, pieces, -0.22, 0.18) if pieces else 1.0
    entries = jax.random.normal(key, dims, jnp.float32) * spread * gain
    return jnp.minimum(jnp.maximum(entries, -limit), limit).astype(kind)


def setup_inputs(seed: int = 0) -> dict:
    key_of = jax.random.split(jax.random.key(seed), 7)
    return {
        "tokens": draw_tokens(jax.random.fold_in(key_of[6], 71), 0),
        "w_query": centred(key_of[1], (D, HEADS * HDIM), D ** -0.5, 0.09375, ((1, 4),)),
        "w_key": centred(key_of[2], (D, HEADS * HDIM), D ** -0.5, 0.09375, ((1, 4),)),
        "w_value": centred(key_of[3], (D, HEADS * HDIM), D ** -0.5, 0.09375, ((1, 4),)),
        "w_out": centred(key_of[4], (HEADS * HDIM, D), (HEADS * HDIM) ** -0.5, 0.125, ((0, 4),)),
        "block_bucket": draw_block_bucket(jax.random.fold_in(key_of[6], 71), 0),
    }


def key_lists(bucket, valid):
    count = bucket.shape[0]
    match = (bucket[:, None] == bucket[None, :]) & valid[None, :]
    rank = jnp.cumsum(match.astype(jnp.int32), axis=1) - 1
    picks = match[:, :, None] & (rank[:, :, None] == jnp.arange(BMAX, dtype=jnp.int32)[None, None, :])
    places = jnp.arange(count, dtype=jnp.int32)[None, :, None]
    index = jnp.sum(jnp.where(picks, places, 0), axis=1).astype(jnp.int32)
    usable = jnp.any(picks, axis=1)
    return index, usable


def attend(query, keys, values, usable):
    scores = jnp.einsum("qhd,khd->hqk", query.astype(jnp.float32), keys.astype(jnp.float32)) * (HDIM ** -0.5)
    scores = jnp.where(usable[None, None, :], scores, -1e30)
    top = jnp.max(scores, axis=-1, keepdims=True)
    expo = jnp.exp(scores - top)
    weights = (expo / jnp.sum(expo, axis=-1, keepdims=True)).astype(jnp.bfloat16)
    mixed = jnp.einsum("hqk,khd->qhd", weights.astype(jnp.float32), values.astype(jnp.float32))
    return mixed.astype(jnp.bfloat16)


def reference(tokens, w_query, w_key, w_value, w_out, block_bucket):
    query = jnp.dot(tokens, w_query, preferred_element_type=jnp.float32).astype(jnp.bfloat16)
    keys = jnp.dot(tokens, w_key, preferred_element_type=jnp.float32).astype(jnp.bfloat16)
    values = jnp.dot(tokens, w_value, preferred_element_type=jnp.float32).astype(jnp.bfloat16)
    query = query.reshape(NBLK, BLOCK, HEADS, HDIM)
    keys = keys.reshape(NBLK, BLOCK, HEADS, HDIM)
    values = values.reshape(NBLK, BLOCK, HEADS, HDIM)
    index, usable = key_lists(block_bucket, jnp.ones((NBLK,), dtype=bool))

    def one_block(which):
        picked = index[which]
        key_rows = jnp.take(keys, picked, axis=0).reshape(BMAX * BLOCK, HEADS, HDIM)
        value_rows = jnp.take(values, picked, axis=0).reshape(BMAX * BLOCK, HEADS, HDIM)
        mask = jnp.repeat(usable[which], BLOCK)
        return attend(query[which], key_rows, value_rows, mask)

    mixed = lax.map(one_block, jnp.arange(NBLK, dtype=jnp.int32))
    mixed = mixed.reshape(TOKENS, HEADS * HDIM)
    return jnp.dot(mixed, w_out, preferred_element_type=jnp.float32).astype(jnp.bfloat16)
```

```python
import jax
import jax.numpy as jnp
from jax import lax
from jax.experimental import pallas as pl
from jax.experimental.pallas import tpu as pltpu
from jax.sharding import PartitionSpec as P

HDIM = 128
SCALE = HDIM ** (-0.5)
BLK = 128
HALF = BLK // 2
NB = 4
FEAT = 1024
WIDTH = 512
PACK = 512
MESH = pl.DeviceIdType.MESH
F32 = jnp.float32
BF16 = jnp.bfloat16


def wrap(n):
    return lax.rem(n + 4, 4)


def kernel(
    ids, tok, wq, wk, wv, wo, out,
    tk, w, acc, qs, s1a, s1b, tx, rel, fin, kvp, wov, wrel, mx,
    idg, idsend, part_v, part_s,
    loc_sem, wloc_sem, tok_s, tok_r, id_s, id_r, ag_s, ag_r, rs_s, rs_r, wo_s, wo_r, mx_s, mx_r,
):
    s = lax.axis_index("seq")
    y = lax.axis_index("head")
    x = s // 8
    z = lax.rem(s // 2, 4)
    c = lax.rem(s, 2)
    s1 = (s1a, s1b)
    started = []

    def place(px, pz, pc):
        return (px * 4 + pz) * 2 + pc

    def ring(axis, k):
        if axis == "y":
            return (s, wrap(y + k))
        if axis == "x":
            return (place(wrap(x + k), z, c), y)
        return (place(x, wrap(z + k), c), y)

    sibling = (place(x, z, 1 - c), y)
    peers = [ring("y", 1), ring("y", -1), sibling]
    peers += [ring(a, k) for a in ("x", "z") for k in (1, 2, 3)]

    def remote(src, dst, send, recv, device):
        copy = pltpu.make_async_remote_copy(
            src_ref=src, dst_ref=dst, send_sem=send, recv_sem=recv,
            device_id=device, device_id_type=MESH,
        )
        copy.start()
        started.append(copy)
        return copy

    tok_local = pltpu.make_async_copy(tok, tk.at[0], loc_sem.at[0])
    tok_local.start()
    w_local = []
    for d in (0, 3, 1, 2):
        rows = pl.ds(pl.multiple_of(wrap(y + d) * FEAT, FEAT), FEAT)
        for j, ref in enumerate((wq, wk, wv)):
            copy = pltpu.make_async_copy(ref.at[rows, :], w.at[d, j], wloc_sem.at[d, j])
            copy.start()
            w_local.append(copy)
    mine = pl.ds(pl.multiple_of(y * FEAT, FEAT), FEAT)
    wo_local = pltpu.make_async_copy(wo.at[:, mine], wov.at[0], loc_sem.at[1])
    wo_local.start()

    barrier = pltpu.get_barrier_semaphore()
    for peer in peers:
        pl.semaphore_signal(barrier, inc=1, device_id=peer, device_id_type=MESH)
    pl.semaphore_wait(barrier, len(peers))

    tok_c = {}
    for i in range(NB):
        rows = pl.ds(i * BLK, BLK)
        tok_c[i, 0] = remote(tok.at[rows, :], tk.at[3, rows, :], tok_s.at[i, 0], tok_r.at[i, 0], ring("y", 1))
        tok_c[i, 1] = remote(tok.at[rows, :], tk.at[1, rows, :], tok_s.at[i, 1], tok_r.at[i, 1], ring("y", -1))

    lane = lax.broadcasted_iota(jnp.int32, (8, 128), 1)
    row = jnp.zeros((8, 128), jnp.int32)
    for i in range(NB):
        row = jnp.where(lane == s * NB + i, ids[i], row)

    def spread(stage, row, targets):
        idsend[stage] = row
        copies = []
        for k, target in targets:
            copies.append(
                remote(idsend.at[stage], idg.at[stage, k - 1], id_s.at[stage, k - 1], id_r.at[stage, k - 1], target)
            )
        return copies

    ids_x = spread(0, row, [(k, ring("x", k)) for k in (1, 2, 3)])

    tok_local.wait()
    for copy in w_local[:3]:
        copy.wait()

    def own_tile(t, carry):
        n, m = t // 2, lax.rem(t, 2)
        rows = pl.ds(pl.multiple_of(m * 256, 256), 256)
        cols = pl.ds(pl.multiple_of(lax.rem(n, 2) * 256, 256), 256)
        acc[n, rows, :] = jnp.dot(tk[0, rows, :], w[0, n // 2, :, cols], preferred_element_type=F32)
        return carry

    lax.fori_loop(0, 12, own_tile, 0)

    for copy in ids_x:
        copy.wait_recv()
    row = row + idg[0, 0] + idg[0, 1] + idg[0, 2]
    ids_z = spread(1, row, [(k, ring("z", k)) for k in (1, 2, 3)])
    for copy in w_local[3:]:
        copy.wait()

    tok_f = {}
    ag = {}
    axes = ("x", "z")

    def forward_tokens(i):
        lo, hi = pl.ds(i * BLK, HALF), pl.ds(i * BLK + HALF, HALF)
        tok_c[i, 0].wait_recv()
        tok_f[i, 0] = remote(tk.at[3, lo, :], tk.at[2, lo, :], tok_s.at[i, 2], tok_r.at[i, 2], ring("y", 1))
        tok_c[i, 1].wait_recv()
        tok_f[i, 1] = remote(tk.at[1, hi, :], tk.at[2, hi, :], tok_s.at[i, 3], tok_r.at[i, 3], ring("y", -1))

    def near_tiles(i):
        rows = pl.ds(i * BLK, BLK)

        def tile(n, carry):
            cols = pl.ds(pl.multiple_of(lax.rem(n, 2) * 256, 256), 256)
            acc[n, rows, :] += jnp.dot(
                tk[3, rows, :], w[3, n // 2, :, cols], preferred_element_type=F32
            ) + jnp.dot(tk[1, rows, :], w[1, n // 2, :, cols], preferred_element_type=F32)
            return carry

        lax.fori_loop(0, 6, tile, 0)

    def far_tiles(i):
        rows = pl.ds(i * BLK, BLK)
        tok_f[i, 0].wait_recv()
        tok_f[i, 1].wait_recv()

        def tile(n, carry):
            cols = pl.ds(pl.multiple_of(lax.rem(n, 2) * 256, 256), 256)
            acc[n, rows, :] += jnp.dot(tk[2, rows, :], w[2, n // 2, :, cols], preferred_element_type=F32)
            return carry

        lax.fori_loop(0, 6, tile, 0)
        for f in range(2):
            qs[f, i] = acc[f, rows, :].astype(BF16)
            s1[f][0, 0, i, :, :256] = acc[2 + f, rows, :].astype(BF16)
            s1[f][0, 0, i, :, 256:] = acc[4 + f, rows, :].astype(BF16)

    def gather_send(i):
        for f in range(2):
            own, a = s1[f].at[0, 0, i], axes[f]
            ag[f, i, 0] = remote(own, s1[f].at[0, 3, i], ag_s.at[f, i, 0], ag_r.at[f, i, 0], ring(a, 1))
            ag[f, i, 1] = remote(own, s1[f].at[0, 1, i], ag_s.at[f, i, 1], ag_r.at[f, i, 1], ring(a, -1))
            ag[f, i, 2] = remote(own, s1[f].at[1, 0, i], ag_s.at[f, i, 2], ag_r.at[f, i, 2], sibling)

    def gather_forward(i):
        lo, hi = pl.ds(0, HALF), pl.ds(HALF, HALF)
        for f in range(2):
            g, a = s1[f], axes[f]
            ag[f, i, 0].wait_recv()
            ag[f, i, 3] = remote(g.at[0, 3, i, lo], g.at[0, 2, i, lo], ag_s.at[f, i, 3], ag_r.at[f, i, 3], ring(a, 1))
            ag[f, i, 5] = remote(g.at[0, 3, i], g.at[1, 3, i], ag_s.at[f, i, 5], ag_r.at[f, i, 5], sibling)
            ag[f, i, 1].wait_recv()
            ag[f, i, 4] = remote(g.at[0, 1, i, hi], g.at[0, 2, i, hi], ag_s.at[f, i, 4], ag_r.at[f, i, 4], ring(a, -1))
            ag[f, i, 6] = remote(g.at[0, 1, i], g.at[1, 1, i], ag_s.at[f, i, 6], ag_r.at[f, i, 6], sibling)

    def gather_far(i):
        for f in range(2):
            g = s1[f]
            ag[f, i, 3].wait_recv()
            ag[f, i, 4].wait_recv()
            ag[f, i, 7] = remote(g.at[0, 2, i], g.at[1, 2, i], ag_s.at[f, i, 7], ag_r.at[f, i, 7], sibling)

    forward_tokens(0)
    near_tiles(0)
    for copy in ids_z:
        copy.wait_recv()
    row = row + idg[1, 0] + idg[1, 1] + idg[1, 2]
    ids_c = spread(2, row, [(1, sibling)])
    forward_tokens(1)
    near_tiles(1)
    far_tiles(0)
    gather_send(0)
    ids_c[0].wait_recv()
    row = row + idg[2, 0]

    across = jnp.broadcast_to(row[0:1, :], (128, 128))
    down = across.T
    one = lax.broadcasted_iota(jnp.int32, (128, 128), 0)
    two = lax.broadcasted_iota(jnp.int32, (128, 128), 1)
    same = (across == down) & (one != two)
    partner = jnp.sum(jnp.where(same, one + 1, 0), axis=0, keepdims=True) - 1
    part_v[...] = jnp.broadcast_to(partner, (8, 128))
    part_copy = pltpu.make_async_copy(part_v, part_s, loc_sem.at[2])
    part_copy.start()

    forward_tokens(2)
    near_tiles(2)
    far_tiles(1)
    gather_send(1)
    gather_forward(0)
    forward_tokens(3)
    near_tiles(3)

    lo = pl.ds(pl.multiple_of(c * 256, 256), 128)
    hi = pl.ds(pl.multiple_of(c * 256 + 128, 128), 128)
    both = pl.ds(pl.multiple_of(c * 256, 256), 256)

    def columns(k):
        return pl.ds(pl.multiple_of(wrap(y + k) * FEAT, FEAT), FEAT)

    wo_c = [
        remote(wo.at[lo, columns(2)], wrel.at[0], wo_s.at[0], wo_r.at[0], ring("y", 1)),
        remote(wo.at[hi, columns(2)], wrel.at[1], wo_s.at[1], wo_r.at[1], ring("y", -1)),
        remote(wo.at[both, columns(1)], wov.at[3, both], wo_s.at[2], wo_r.at[2], ring("y", 1)),
        remote(wo.at[both, columns(-1)], wov.at[1, both], wo_s.at[3], wo_r.at[3], ring("y", -1)),
    ]
    far_tiles(2)
    gather_send(2)
    gather_forward(1)
    gather_far(0)
    far_tiles(3)
    gather_send(3)
    gather_forward(2)
    gather_far(1)
    gather_forward(3)
    gather_far(2)
    wo_c[0].wait_recv()
    wo_f0 = remote(wrel.at[0], wov.at[2, lo], wo_s.at[4], wo_r.at[4], ring("y", 1))
    wo_c[1].wait_recv()
    wo_f1 = remote(wrel.at[1], wov.at[2, hi], wo_s.at[5], wo_r.at[5], ring("y", -1))
    gather_far(3)
    part_copy.wait()

    def choice(f, k, i):
        dest = place(x, wrap(z + k), c) if f == 0 else place(wrap(x + k), z, c)
        p = part_s[0, dest * NB + i]
        at = jnp.maximum(p, 0)
        xp, zp = at // 32, lax.rem(at // 8, 4)
        cp, ip = lax.rem(at // 4, 2), lax.rem(at, 4)
        along, held = (xp - x, zp) if f == 0 else (zp - z, xp)
        return (lax.rem(cp + c, 2), wrap(along), ip), held, p

    second = ("z", "x")
    here = (z, x)
    for f in range(2):
        for i in range(NB):
            for k in (2, 5, 6, 7):
                ag[f, i, k].wait_recv()

    def fill(f, g, k, slots, relay=None):
        for n, i in enumerate(slots):
            index, held, _ = choice(f, k, i)
            packet = s1[f][index[0], index[1], index[2]]
            if relay is not None:
                packet = jnp.where(held == here[f], packet, rel[f, relay, n])
            tx[f, g, n] = packet

    rs = {}
    for f in range(2):
        right, left = ring(second[f], 1), ring(second[f], -1)
        fill(f, 0, 2, (0, 1))
        rs[f, 0] = remote(tx.at[f, 0], rel.at[f, 0], rs_s.at[f, 0], rs_r.at[f, 0], right)
        fill(f, 1, 2, (2, 3))
        rs[f, 1] = remote(tx.at[f, 1], rel.at[f, 1], rs_s.at[f, 1], rs_r.at[f, 1], left)
    for f in range(2):
        right, left = ring(second[f], 1), ring(second[f], -1)
        fill(f, 2, 1, (2, 3))
        rs[f, 2] = remote(tx.at[f, 2], fin.at[f, 0, pl.ds(2, 2)], rs_s.at[f, 2], rs_r.at[f, 2], right)
        fill(f, 3, -1, (0, 1))
        rs[f, 3] = remote(tx.at[f, 3], fin.at[f, 1, pl.ds(0, 2)], rs_s.at[f, 3], rs_r.at[f, 3], left)
    for f in range(2):
        right, left = ring(second[f], 1), ring(second[f], -1)
        rs[f, 0].wait_recv()
        fill(f, 4, 1, (0, 1), 0)
        rs[f, 4] = remote(tx.at[f, 4], fin.at[f, 0, pl.ds(0, 2)], rs_s.at[f, 4], rs_r.at[f, 4], right)
        rs[f, 1].wait_recv()
        fill(f, 5, -1, (2, 3), 1)
        rs[f, 5] = remote(tx.at[f, 5], fin.at[f, 1, pl.ds(2, 2)], rs_s.at[f, 5], rs_r.at[f, 5], left)

    wo_x = []
    for n, (d, ready) in enumerate(((3, wo_c[2:3]), (1, wo_c[3:4]), (2, [wo_f0, wo_f1]))):
        for copy in ready:
            copy.wait_recv()
        wo_x.append(remote(wov.at[d, both], wov.at[d, both], wo_s.at[6 + n], wo_r.at[6 + n], sibling))

    def attend(i):
        rows = pl.ds(i * BLK, BLK)
        for f in range(2):
            index, held, p = choice(f, 0, i)
            from_left = (held == wrap(here[f] - 1)) | ((held == wrap(here[f] + 2)) & (i < 2))
            packet = jnp.where(from_left, fin[f, 0, i], fin[f, 1, i])
            kvp[f] = jnp.where(held == here[f], s1[f][index[0], index[1], index[2]], packet)
            for j in range(2):
                kc, vc = pl.ds(j * HDIM, HDIM), pl.ds(256 + j * HDIM, HDIM)
                query = qs[f, i, :, kc]
                dims = (((1,), (1,)), ((), ()))
                near = lax.dot_general(query, s1[f][0, 0, i, :, kc], dims, preferred_element_type=F32) * SCALE
                far = lax.dot_general(query, kvp[f, :, kc], dims, preferred_element_type=F32) * SCALE
                far = jnp.where(p >= 0, far, -1e30)
                top = jnp.maximum(jnp.max(near, axis=1, keepdims=True), jnp.max(far, axis=1, keepdims=True))
                near, far = jnp.exp(near - top), jnp.exp(far - top)
                total = jnp.sum(near, axis=1, keepdims=True) + jnp.sum(far, axis=1, keepdims=True)
                near, far = (near / total).astype(BF16), (far / total).astype(BF16)
                mixed = jnp.dot(near, s1[f][0, 0, i, :, vc], preferred_element_type=F32)
                mixed += jnp.dot(far, kvp[f, :, vc], preferred_element_type=F32)
                mx[0, rows, pl.ds((2 * f + j) * HDIM, HDIM)] = mixed.astype(BF16)

    for f in range(2):
        for g in (2, 3, 4, 5):
            rs[f, g].wait_recv()

    mx_c = {}

    def send_mixed(i):
        rows = pl.ds(i * BLK, BLK)
        mx_c[i, 0] = remote(mx.at[0, rows], mx.at[3, rows], mx_s.at[i, 0], mx_r.at[i, 0], ring("y", 1))
        mx_c[i, 1] = remote(mx.at[0, rows], mx.at[1, rows], mx_s.at[i, 1], mx_r.at[i, 1], ring("y", -1))

    def forward_mixed(i):
        lo, hi = pl.ds(i * BLK, HALF), pl.ds(i * BLK + HALF, HALF)
        mx_c[i, 0].wait_recv()
        mx_c[i, 2] = remote(mx.at[3, lo], mx.at[2, lo], mx_s.at[i, 2], mx_r.at[i, 2], ring("y", 1))
        mx_c[i, 1].wait_recv()
        mx_c[i, 3] = remote(mx.at[1, hi], mx.at[2, hi], mx_s.at[i, 3], mx_r.at[i, 3], ring("y", -1))

    def project(i):
        rows = pl.ds(i * BLK, BLK)
        mx_c[i, 2].wait_recv()
        mx_c[i, 3].wait_recv()

        def tile(n, carry):
            cols = pl.ds(pl.multiple_of(n * 256, 256), 256)
            total = jnp.dot(mx[0, rows, :], wov[0, :, cols], preferred_element_type=F32)
            for d in (1, 2, 3):
                total += jnp.dot(mx[d, rows, :], wov[d, :, cols], preferred_element_type=F32)
            out[rows, cols] = total.astype(BF16)
            return carry

        lax.fori_loop(0, 4, tile, 0)

    for i in range(NB):
        attend(i)
        send_mixed(i)
        if i:
            forward_mixed(i - 1)
    forward_mixed(NB - 1)
    wo_local.wait()
    for copy in wo_x:
        copy.wait_recv()
    for i in range(NB):
        project(i)
    for copy in started:
        copy.wait_send()


def per_device(tokens, w_query, w_key, w_value, w_out, block_bucket):
    anywhere = pl.BlockSpec(memory_space=pl.ANY)
    dma = pltpu.SemaphoreType.DMA
    return pl.pallas_call(
        kernel,
        out_shape=jax.ShapeDtypeStruct((NB * BLK, FEAT), BF16),
        in_specs=[pl.BlockSpec(memory_space=pltpu.SMEM)] + [anywhere] * 5,
        out_specs=pl.BlockSpec(memory_space=pltpu.VMEM),
        scratch_shapes=[
            pltpu.VMEM((4, NB * BLK, FEAT), BF16),
            pltpu.VMEM((4, 3, FEAT, WIDTH), BF16),
            pltpu.VMEM((6, NB * BLK, 256), F32),
            pltpu.VMEM((2, NB, BLK, 256), BF16),
            pltpu.VMEM((2, 4, NB, BLK, PACK), BF16),
            pltpu.VMEM((2, 4, NB, BLK, PACK), BF16),
            pltpu.VMEM((2, 6, 2, BLK, PACK), BF16),
            pltpu.VMEM((2, 2, 2, BLK, PACK), BF16),
            pltpu.VMEM((2, 2, NB, BLK, PACK), BF16),
            pltpu.VMEM((2, BLK, PACK), BF16),
            pltpu.VMEM((4, WIDTH, FEAT), BF16),
            pltpu.VMEM((2, 128, FEAT), BF16),
            pltpu.VMEM((4, NB * BLK, WIDTH), BF16),
            pltpu.VMEM((3, 3, 8, 128), jnp.int32),
            pltpu.VMEM((3, 8, 128), jnp.int32),
            pltpu.VMEM((8, 128), jnp.int32),
            pltpu.SMEM((8, 128), jnp.int32),
            dma((3,)),
            dma((4, 3)),
            dma((NB, 4)),
            dma((NB, 4)),
            dma((3, 3)),
            dma((3, 3)),
            dma((2, NB, 8)),
            dma((2, NB, 8)),
            dma((2, 6)),
            dma((2, 6)),
            dma((9,)),
            dma((9,)),
            dma((NB, 4)),
            dma((NB, 4)),
        ],
        compiler_params=pltpu.CompilerParams(
            collective_id=0, has_side_effects=True, vmem_limit_bytes=58 * 2**20
        ),
    )(block_bucket, tokens, w_query, w_key, w_value, w_out)


def solution(mesh):
    placed = (
        P("seq", "head"),
        P(None, "head"),
        P(None, "head"),
        P(None, "head"),
        P("head", None),
        P("seq"),
    )
    return jax.shard_map(
        per_device, mesh=mesh, in_specs=placed, out_specs=P("seq", "head"), check_vma=False
    )
```

```python
import jax
import jax.numpy as jnp
from jax import lax
from jax.experimental import pallas as pl
from jax.experimental.pallas import tpu as pltpu
from jax.sharding import PartitionSpec as P

HDIM = 128
SCALE = HDIM ** (-0.5)
BLK = 128
HALF = BLK // 2
NB = 4
FEAT = 1024
WIDTH = 512
PACK = 512
MESH = pl.DeviceIdType.MESH
F32 = jnp.float32
BF16 = jnp.bfloat16


def wrap(n):
    return lax.rem(n + 4, 4)


def kernel(
    ids, tok, wq, wk, wv, wo, out,
    tk, w, acc, qs, s1a, s1b, tx, rel, fin, kvp, wov, mx,
    idg, idsend, part_v, part_s,
    loc_sem, wloc_sem, tok_s, tok_r, id_s, id_r, ag_s, ag_r, rs_s, rs_r, wo_s, wo_r, mx_s, mx_r,
):
    s = lax.axis_index("seq")
    y = lax.axis_index("head")
    x = s // 8
    z = lax.rem(s // 2, 4)
    c = lax.rem(s, 2)
    s1 = (s1a, s1b)
    wo6 = wo.reshape(4, 4, 2, 16, 4 * FEAT)
    started = []

    def place(px, pz, pc):
        return (px * 4 + pz) * 2 + pc

    def ring(axis, k):
        if axis == "y":
            return (s, wrap(y + k))
        if axis == "x":
            return (place(wrap(x + k), z, c), y)
        return (place(x, wrap(z + k), c), y)

    sibling = (place(x, z, 1 - c), y)
    peers = [sibling] + [ring(a, k) for a in ("y", "x", "z") for k in (1, 2, 3)]

    def remote(src, dst, send, recv, device):
        copy = pltpu.make_async_remote_copy(
            src_ref=src, dst_ref=dst, send_sem=send, recv_sem=recv,
            device_id=device, device_id_type=MESH,
        )
        copy.start()
        started.append(copy)
        return copy

    tok_local = pltpu.make_async_copy(tok, tk.at[0], loc_sem.at[0])
    tok_local.start()
    w_local = []
    for d in (0, 3, 1, 2):
        rows = pl.ds(pl.multiple_of(wrap(y + d) * FEAT, FEAT), FEAT)
        for j, ref in enumerate((wq, wk, wv)):
            copy = pltpu.make_async_copy(ref.at[rows, :], w.at[d, j], wloc_sem.at[d, j])
            copy.start()
            w_local.append(copy)
    mine = pl.ds(pl.multiple_of(y * FEAT, FEAT), FEAT)
    wo_local = pltpu.make_async_copy(wo6.at[:, :, :, :, mine], wov.at[0], loc_sem.at[1])
    wo_local.start()

    barrier = pltpu.get_barrier_semaphore()
    for peer in peers:
        pl.semaphore_signal(barrier, inc=1, device_id=peer, device_id_type=MESH)
    pl.semaphore_wait(barrier, len(peers))

    wo_y = []
    row16 = pl.ds(pl.multiple_of(s * 16, 16), 16)
    for k in (1, 2, 3):
        cols = pl.ds(pl.multiple_of(wrap(y + k) * FEAT, FEAT), FEAT)
        wo_y.append(remote(wo.at[row16, cols], wov.at[4 - k, x, z, c], wo_s.at[k - 1], wo_r.at[k - 1], ring("y", k)))

    tok_c = {}
    tok_f = {}

    def send_tokens(k):
        rows = pl.ds(k * HALF, HALF)
        tok_c[k, 0] = remote(tok.at[rows, :], tk.at[3, rows, :], tok_s.at[k, 0], tok_r.at[k, 0], ring("y", 1))
        tok_c[k, 1] = remote(tok.at[rows, :], tk.at[1, rows, :], tok_s.at[k, 1], tok_r.at[k, 1], ring("y", -1))

    def tokens_event(k):
        lo, hi = pl.ds(k * HALF, HALF // 2), pl.ds(k * HALF + HALF // 2, HALF // 2)
        tok_c[k, 0].wait_recv()
        tok_f[k, 0] = remote(tk.at[3, lo, :], tk.at[2, lo, :], tok_s.at[k, 2], tok_r.at[k, 2], ring("y", 1))
        tok_c[k, 1].wait_recv()
        tok_f[k, 1] = remote(tk.at[1, hi, :], tk.at[2, hi, :], tok_s.at[k, 3], tok_r.at[k, 3], ring("y", -1))
        if k + 2 < 8:
            send_tokens(k + 2)

    send_tokens(0)
    send_tokens(1)

    lane = lax.broadcasted_iota(jnp.int32, (8, 128), 1)
    row = jnp.zeros((8, 128), jnp.int32)
    for i in range(NB):
        row = jnp.where(lane == s * NB + i, ids[i], row)

    def spread(stage, row, targets):
        idsend[stage] = row
        copies = []
        for k, target in targets:
            copies.append(
                remote(idsend.at[stage], idg.at[stage, k - 1], id_s.at[stage, k - 1], id_r.at[stage, k - 1], target)
            )
        return copies

    ids_x = spread(0, row, [(k, ring("x", k)) for k in (1, 2, 3)])

    tok_local.wait()
    for copy in w_local[:3]:
        copy.wait()

    def own_tile(t, carry):
        n, m = t // 2, lax.rem(t, 2)
        rows = pl.ds(pl.multiple_of(m * 256, 256), 256)
        cols = pl.ds(pl.multiple_of(lax.rem(n, 2) * 256, 256), 256)
        acc[n, rows, :] = jnp.dot(tk[0, rows, :], w[0, n // 2, :, cols], preferred_element_type=F32)
        return carry

    lax.fori_loop(0, 12, own_tile, 0)

    def near_tiles(i):
        rows = pl.ds(i * BLK, BLK)

        def tile(n, carry):
            cols = pl.ds(pl.multiple_of(lax.rem(n, 2) * 256, 256), 256)
            acc[n, rows, :] += jnp.dot(
                tk[3, rows, :], w[3, n // 2, :, cols], preferred_element_type=F32
            ) + jnp.dot(tk[1, rows, :], w[1, n // 2, :, cols], preferred_element_type=F32)
            return carry

        lax.fori_loop(0, 6, tile, 0)

    def far_tiles(i, first, last):
        rows = pl.ds(i * BLK, BLK)

        def tile(n, carry):
            cols = pl.ds(pl.multiple_of(lax.rem(n, 2) * 256, 256), 256)
            acc[n, rows, :] += jnp.dot(tk[2, rows, :], w[2, n // 2, :, cols], preferred_element_type=F32)
            return carry

        lax.fori_loop(first, last, tile, 0)

    ag = {}
    axes = ("x", "z")

    def finish_keys(i):
        rows = pl.ds(i * BLK, BLK)
        for k in (2 * i, 2 * i + 1):
            tok_f[k, 0].wait_recv()
            tok_f[k, 1].wait_recv()
        far_tiles(i, 2, 6)
        for f in range(2):
            s1[f][0, 0, i, :, :256] = acc[2 + f, rows, :].astype(BF16)
            s1[f][0, 0, i, :, 256:] = acc[4 + f, rows, :].astype(BF16)
        for f in range(2):
            own, a = s1[f].at[0, 0, i], axes[f]
            for n, (k, d) in enumerate(((2, 2), (1, 3), (-1, 1))):
                ag[f, i, d] = remote(own, s1[f].at[0, d, i], ag_s.at[f, i, n], ag_r.at[f, i, n], ring(a, k))
            ag[f, i, "own"] = remote(own, s1[f].at[1, 0, i], ag_s.at[f, i, 3], ag_r.at[f, i, 3], sibling)

    def finish_query(i):
        rows = pl.ds(i * BLK, BLK)
        far_tiles(i, 0, 2)
        for f in range(2):
            qs[f, i] = acc[f, rows, :].astype(BF16)

    def to_sibling(i):
        for n, d in ((0, 3), (1, 1), (2, 2)):
            for f in range(2):
                ag[f, i, d].wait_recv()
                ag[f, i, "s", d] = remote(
                    s1[f].at[0, d, i], s1[f].at[1, d, i], ag_s.at[f, i, 4 + n], ag_r.at[f, i, 4 + n], sibling
                )

    for copy in ids_x:
        copy.wait_recv()
    row = row + idg[0, 0] + idg[0, 1] + idg[0, 2]
    ids_z = spread(1, row, [(k, ring("z", k)) for k in (1, 2, 3)])

    for copy in wo_y:
        copy.wait_recv()
    left_cols, right_cols = pl.ds(0, 512), pl.ds(512, 512)
    three = pl.ds(1, 3)
    wo_1 = []
    for k in (2, 1, 3):
        own = wov.at[three, x, z, c, :, left_cols]
        wo_1.append(remote(own, own, wo_s.at[2 + k], wo_r.at[2 + k], ring("x", k)))
        own = wov.at[three, x, z, c, :, right_cols]
        wo_1.append(remote(own, own, wo_s.at[5 + k], wo_r.at[5 + k], ring("z", k)))

    tokens_event(0)
    for copy in w_local[3:]:
        copy.wait()
    for copy in ids_z:
        copy.wait_recv()
    row = row + idg[1, 0] + idg[1, 1] + idg[1, 2]
    ids_c = spread(2, row, [(1, sibling)])
    tokens_event(1)

    for copy in wo_1:
        copy.wait_recv()
    wo_2 = []
    for k in (2, 1, 3):
        own = wov.at[three, :, z, c, :, left_cols]
        wo_2.append(remote(own, own, wo_s.at[8 + k], wo_r.at[8 + k], ring("z", k)))
        own = wov.at[three, x, :, c, :, right_cols]
        wo_2.append(remote(own, own, wo_s.at[11 + k], wo_r.at[11 + k], ring("x", k)))

    near_tiles(0)
    ids_c[0].wait_recv()
    row = row + idg[2, 0]

    across = jnp.broadcast_to(row[0:1, :], (128, 128))
    down = across.T
    one = lax.broadcasted_iota(jnp.int32, (128, 128), 0)
    two = lax.broadcasted_iota(jnp.int32, (128, 128), 1)
    same = (across == down) & (one != two)
    partner = jnp.sum(jnp.where(same, one + 1, 0), axis=0, keepdims=True) - 1
    part_v[...] = jnp.broadcast_to(partner, (8, 128))
    part_copy = pltpu.make_async_copy(part_v, part_s, loc_sem.at[2])
    part_copy.start()

    tokens_event(2)
    finish_keys(0)
    tokens_event(3)
    finish_query(0)
    near_tiles(1)
    tokens_event(4)
    finish_keys(1)
    for copy in wo_2:
        copy.wait_recv()
    own = wov.at[three, :, :, c]
    wo_3 = remote(own, own, wo_s.at[15], wo_r.at[15], sibling)
    tokens_event(5)
    near_tiles(2)
    to_sibling(0)
    tokens_event(6)
    finish_query(1)
    finish_keys(2)
    tokens_event(7)
    near_tiles(3)
    to_sibling(1)
    finish_keys(3)
    finish_query(2)
    to_sibling(2)
    finish_query(3)
    part_copy.wait()
    to_sibling(3)

    def choice(f, k, i):
        dest = place(x, wrap(z + k), c) if f == 0 else place(wrap(x + k), z, c)
        p = part_s[0, dest * NB + i]
        at = jnp.maximum(p, 0)
        xp, zp = at // 32, lax.rem(at // 8, 4)
        cp, ip = lax.rem(at // 4, 2), lax.rem(at, 4)
        along, held = (xp - x, zp) if f == 0 else (zp - z, xp)
        return (lax.rem(cp + c, 2), wrap(along), ip), held, p

    second = ("z", "x")
    here = (z, x)
    for f in range(2):
        for i in range(NB):
            ag[f, i, "own"].wait_recv()
            for d in (1, 2, 3):
                ag[f, i, "s", d].wait_recv()

    low, high = pl.ds(0, HALF), pl.ds(HALF, HALF)
    rs = {}

    def pass_on(f, i, g, k, rows, to, dst, relay=None):
        index, held, _ = choice(f, k, i)
        packet = s1[f][index[0], index[1], index[2], rows]
        if relay is not None:
            packet = jnp.where(held == here[f], packet, rel[f, i, relay])
        tx[f, i, g] = packet
        rs[f, i, g] = remote(tx.at[f, i, g], dst, rs_s.at[f, i, g], rs_r.at[f, i, g], ring(second[f], to))

    def relay_out(i):
        for f in range(2):
            pass_on(f, i, 0, 2, low, 1, rel.at[f, i, 0])
            pass_on(f, i, 1, 2, high, -1, rel.at[f, i, 1])

    def direct_out(i):
        for f in range(2):
            pass_on(f, i, 2, 1, high, 1, fin.at[f, 0, i, high])
            pass_on(f, i, 3, -1, low, -1, fin.at[f, 1, i, low])

    def merged_out(i):
        for f in range(2):
            rs[f, i, 0].wait_recv()
            pass_on(f, i, 4, 1, low, 1, fin.at[f, 0, i, low], 0)
            rs[f, i, 1].wait_recv()
            pass_on(f, i, 5, -1, high, -1, fin.at[f, 1, i, high], 1)

    def attend(i):
        rows = pl.ds(i * BLK, BLK)
        for f in range(2):
            for g in (2, 3, 4, 5):
                rs[f, i, g].wait_recv()
        for f in range(2):
            index, held, p = choice(f, 0, i)
            at_left, at_right = held == wrap(here[f] - 1), held == wrap(here[f] + 1)
            for half, from_left in ((low, jnp.logical_not(at_right)), (high, at_left)):
                packet = jnp.where(from_left, fin[f, 0, i, half], fin[f, 1, i, half])
                own = s1[f][index[0], index[1], index[2], half]
                kvp[f, half] = jnp.where(held == here[f], own, packet)
            for j in range(2):
                kc, vc = pl.ds(j * HDIM, HDIM), pl.ds(256 + j * HDIM, HDIM)
                query = qs[f, i, :, kc]
                dims = (((1,), (1,)), ((), ()))
                near = lax.dot_general(query, s1[f][0, 0, i, :, kc], dims, preferred_element_type=F32) * SCALE
                far = lax.dot_general(query, kvp[f, :, kc], dims, preferred_element_type=F32) * SCALE
                far = jnp.where(p >= 0, far, -1e30)
                top = jnp.maximum(jnp.max(near, axis=1, keepdims=True), jnp.max(far, axis=1, keepdims=True))
                near, far = jnp.exp(near - top), jnp.exp(far - top)
                total = jnp.sum(near, axis=1, keepdims=True) + jnp.sum(far, axis=1, keepdims=True)
                near, far = (near / total).astype(BF16), (far / total).astype(BF16)
                mixed = jnp.dot(near, s1[f][0, 0, i, :, vc], preferred_element_type=F32)
                mixed += jnp.dot(far, kvp[f, :, vc], preferred_element_type=F32)
                mx[0, rows, pl.ds((2 * f + j) * HDIM, HDIM)] = mixed.astype(BF16)

    mx_c = {}

    def send_mixed(i):
        rows = pl.ds(i * BLK, BLK)
        if i == NB - 1:
            mx_c[i, 2] = remote(mx.at[0, rows], mx.at[2, rows], mx_s.at[i, 2], mx_r.at[i, 2], ring("y", 2))
        mx_c[i, 0] = remote(mx.at[0, rows], mx.at[3, rows], mx_s.at[i, 0], mx_r.at[i, 0], ring("y", 1))
        mx_c[i, 1] = remote(mx.at[0, rows], mx.at[1, rows], mx_s.at[i, 1], mx_r.at[i, 1], ring("y", -1))

    def forward_mixed(i):
        lo, hi = pl.ds(i * BLK, HALF), pl.ds(i * BLK + HALF, HALF)
        mx_c[i, 0].wait_recv()
        mx_c[i, 2] = remote(mx.at[3, lo], mx.at[2, lo], mx_s.at[i, 2], mx_r.at[i, 2], ring("y", 1))
        mx_c[i, 1].wait_recv()
        mx_c[i, 3] = remote(mx.at[1, hi], mx.at[2, hi], mx_s.at[i, 3], mx_r.at[i, 3], ring("y", -1))

    def project(i):
        rows = pl.ds(i * BLK, BLK)
        for n in (0, 1, 2) if i == NB - 1 else (2, 3):
            mx_c[i, n].wait_recv()

        def tile(n, carry):
            cols = pl.ds(pl.multiple_of(n * 256, 256), 256)
            total = jnp.dot(mx[0, rows, :], wov[0, :, :, :, :, cols].reshape(WIDTH, 256), preferred_element_type=F32)
            for d in (1, 2, 3):
                part = wov[d, :, :, :, :, cols].reshape(WIDTH, 256)
                total += jnp.dot(mx[d, rows, :], part, preferred_element_type=F32)
            out[rows, cols] = total.astype(BF16)
            return carry

        lax.fori_loop(0, 4, tile, 0)

    relay_out(0)
    direct_out(0)
    relay_out(1)
    merged_out(0)
    direct_out(1)
    relay_out(2)
    merged_out(1)
    direct_out(2)
    relay_out(3)
    attend(0)
    send_mixed(0)
    merged_out(2)
    direct_out(3)
    attend(1)
    send_mixed(1)
    merged_out(3)
    forward_mixed(0)
    attend(2)
    send_mixed(2)
    forward_mixed(1)
    attend(3)
    send_mixed(3)
    forward_mixed(2)
    wo_local.wait()
    wo_3.wait_recv()
    for i in range(NB):
        project(i)
    for copy in started:
        copy.wait_send()


def per_device(tokens, w_query, w_key, w_value, w_out, block_bucket):
    anywhere = pl.BlockSpec(memory_space=pl.ANY)
    dma = pltpu.SemaphoreType.DMA
    return pl.pallas_call(
        kernel,
        out_shape=jax.ShapeDtypeStruct((NB * BLK, FEAT), BF16),
        in_specs=[pl.BlockSpec(memory_space=pltpu.SMEM)] + [anywhere] * 5,
        out_specs=pl.BlockSpec(memory_space=pltpu.VMEM),
        scratch_shapes=[
            pltpu.VMEM((4, NB * BLK, FEAT), BF16),
            pltpu.VMEM((4, 3, FEAT, WIDTH), BF16),
            pltpu.VMEM((6, NB * BLK, 256), F32),
            pltpu.VMEM((2, NB, BLK, 256), BF16),
            pltpu.VMEM((2, 4, NB, BLK, PACK), BF16),
            pltpu.VMEM((2, 4, NB, BLK, PACK), BF16),
            pltpu.VMEM((2, NB, 6, HALF, PACK), BF16),
            pltpu.VMEM((2, NB, 2, HALF, PACK), BF16),
            pltpu.VMEM((2, 2, NB, BLK, PACK), BF16),
            pltpu.VMEM((2, BLK, PACK), BF16),
            pltpu.VMEM((4, 4, 4, 2, 16, FEAT), BF16),
            pltpu.VMEM((4, NB * BLK, WIDTH), BF16),
            pltpu.VMEM((3, 3, 8, 128), jnp.int32),
            pltpu.VMEM((3, 8, 128), jnp.int32),
            pltpu.VMEM((8, 128), jnp.int32),
            pltpu.SMEM((8, 128), jnp.int32),
            dma((3,)),
            dma((4, 3)),
            dma((2 * NB, 4)),
            dma((2 * NB, 4)),
            dma((3, 3)),
            dma((3, 3)),
            dma((2, NB, 7)),
            dma((2, NB, 7)),
            dma((2, NB, 6)),
            dma((2, NB, 6)),
            dma((16,)),
            dma((16,)),
            dma((NB, 4)),
            dma((NB, 4)),
        ],
        compiler_params=pltpu.CompilerParams(
            collective_id=0, has_side_effects=True, vmem_limit_bytes=58 * 2**20
        ),
    )(block_bucket, tokens, w_query, w_key, w_value, w_out)


def solution(mesh):
    placed = (
        P("seq", "head"),
        P(None, "head"),
        P(None, "head"),
        P(None, "head"),
        P("head", None),
        P("seq"),
    )
    return jax.shard_map(
        per_device, mesh=mesh, in_specs=placed, out_specs=P("seq", "head"), check_vma=False
    )
```

```python
import jax
import jax.numpy as jnp
from jax import lax
from jax.experimental import pallas as pl
from jax.experimental.pallas import tpu as pltpu
from jax.sharding import PartitionSpec as P

HDIM = 128
SCALE = HDIM ** (-0.5)
BLK = 128
HALF = BLK // 2
NB = 4
FEAT = 1024
WIDTH = 512
PACK = 512
MESH = pl.DeviceIdType.MESH
F32 = jnp.float32
BF16 = jnp.bfloat16


def wrap(n):
    return lax.rem(n + 4, 4)


def kernel(
    ids, tok, wq, wk, wv, wo, out,
    tk, w, acc, qs, s1a, s1b, tx, rel, fin, kvp, wov, mx,
    idg, idsend, part_v, part_s,
    loc_sem, wloc_sem, tok_s, tok_r, id_s, id_r, ag_s, ag_r, rs_s, rs_r, wo_s, wo_r, mx_s, mx_r,
):
    s = lax.axis_index("seq")
    y = lax.axis_index("head")
    x = s // 8
    z = lax.rem(s // 2, 4)
    c = lax.rem(s, 2)
    s1 = (s1a, s1b)
    wo6 = wo.reshape(4, 4, 2, 16, 4 * FEAT)
    started = []

    def place(px, pz, pc):
        return (px * 4 + pz) * 2 + pc

    def ring(axis, k):
        if axis == "y":
            return (s, wrap(y + k))
        if axis == "x":
            return (place(wrap(x + k), z, c), y)
        return (place(x, wrap(z + k), c), y)

    sibling = (place(x, z, 1 - c), y)
    peers = [sibling] + [ring(a, k) for a in ("y", "x", "z") for k in (1, 2, 3)]

    def remote(src, dst, send, recv, device):
        copy = pltpu.make_async_remote_copy(
            src_ref=src, dst_ref=dst, send_sem=send, recv_sem=recv,
            device_id=device, device_id_type=MESH,
        )
        copy.start()
        started.append(copy)
        return copy

    barrier = pltpu.get_barrier_semaphore()
    for peer in peers:
        pl.semaphore_signal(barrier, inc=1, device_id=peer, device_id_type=MESH)

    tok_local = pltpu.make_async_copy(tok, tk.at[0], loc_sem.at[0])
    tok_local.start()
    w_local = []
    for d in (0, 3, 1, 2):
        rows = pl.ds(pl.multiple_of(wrap(y + d) * FEAT, FEAT), FEAT)
        for j, ref in enumerate((wq, wk, wv)):
            copy = pltpu.make_async_copy(ref.at[rows, :], w.at[d, j], wloc_sem.at[d, j])
            copy.start()
            w_local.append(copy)
    mine = pl.ds(pl.multiple_of(y * FEAT, FEAT), FEAT)
    wo_local = pltpu.make_async_copy(wo6.at[:, :, :, :, mine], wov.at[0], loc_sem.at[1])
    wo_local.start()

    pl.semaphore_wait(barrier, len(peers))

    wo_y = []
    row16 = pl.ds(pl.multiple_of(s * 16, 16), 16)
    for k in (1, 2, 3):
        cols = pl.ds(pl.multiple_of(wrap(y + k) * FEAT, FEAT), FEAT)
        wo_y.append(remote(wo.at[row16, cols], wov.at[4 - k, x, z, c], wo_s.at[k - 1], wo_r.at[k - 1], ring("y", k)))

    tok_c = {}
    tok_f = {}

    def send_tokens(k):
        rows = pl.ds(k * HALF, HALF)
        tok_c[k, 0] = remote(tok.at[rows, :], tk.at[3, rows, :], tok_s.at[k, 0], tok_r.at[k, 0], ring("y", 1))
        tok_c[k, 1] = remote(tok.at[rows, :], tk.at[1, rows, :], tok_s.at[k, 1], tok_r.at[k, 1], ring("y", -1))

    def tokens_event(k):
        lo, hi = pl.ds(k * HALF, HALF // 2), pl.ds(k * HALF + HALF // 2, HALF // 2)
        tok_c[k, 0].wait_recv()
        if k < 7:
            tok_f[k, 0] = remote(tk.at[3, lo, :], tk.at[2, lo, :], tok_s.at[k, 2], tok_r.at[k, 2], ring("y", 1))
        tok_c[k, 1].wait_recv()
        if k < 7:
            tok_f[k, 1] = remote(tk.at[1, hi, :], tk.at[2, hi, :], tok_s.at[k, 3], tok_r.at[k, 3], ring("y", -1))
        if k + 2 < 8:
            send_tokens(k + 2)
        if k == 6:
            rows = pl.ds(7 * HALF, HALF)
            tok_f[7, 0] = remote(tok.at[rows, :], tk.at[2, rows, :], tok_s.at[7, 2], tok_r.at[7, 2], ring("y", 2))

    send_tokens(0)
    send_tokens(1)

    lane = lax.broadcasted_iota(jnp.int32, (8, 128), 1)
    row = jnp.zeros((8, 128), jnp.int32)
    for i in range(NB):
        row = jnp.where(lane == s * NB + i, ids[i], row)

    def spread(stage, row, targets):
        idsend[stage] = row
        copies = []
        for k, target in targets:
            copies.append(
                remote(idsend.at[stage], idg.at[stage, k - 1], id_s.at[stage, k - 1], id_r.at[stage, k - 1], target)
            )
        return copies

    ids_x = spread(0, row, [(k, ring("x", k)) for k in (1, 2, 3)])

    tok_local.wait()
    for copy in w_local[:3]:
        copy.wait()

    def own_tile(t, carry):
        n, m = t // 2, lax.rem(t, 2)
        rows = pl.ds(pl.multiple_of(m * 256, 256), 256)
        cols = pl.ds(pl.multiple_of(lax.rem(n, 2) * 256, 256), 256)
        acc[n, rows, :] = jnp.dot(tk[0, rows, :], w[0, n // 2, :, cols], preferred_element_type=F32)
        return carry

    lax.fori_loop(0, 12, own_tile, 0)

    def near_tiles(i):
        rows = pl.ds(i * BLK, BLK)

        def tile(n, carry):
            cols = pl.ds(pl.multiple_of(lax.rem(n, 2) * 256, 256), 256)
            acc[n, rows, :] += jnp.dot(
                tk[3, rows, :], w[3, n // 2, :, cols], preferred_element_type=F32
            ) + jnp.dot(tk[1, rows, :], w[1, n // 2, :, cols], preferred_element_type=F32)
            return carry

        lax.fori_loop(0, 6, tile, 0)

    pieces = ((0, 0, BLK), (1, 0, BLK), (2, 0, HALF), (2, HALF, HALF), (3, 0, HALF), (3, HALF, HALF))

    def far_tiles(start, count, first, last):
        rows = pl.ds(start, count)

        def tile(n, carry):
            cols = pl.ds(pl.multiple_of(lax.rem(n, 2) * 256, 256), 256)
            acc[n, rows, :] += jnp.dot(tk[2, rows, :], w[2, n // 2, :, cols], preferred_element_type=F32)
            return carry

        lax.fori_loop(first, last, tile, 0)

    ag = {}
    axes = ("x", "z")

    def finish_keys(p):
        i, start, count = pieces[p]
        rows, part = pl.ds(i * BLK + start, count), pl.ds(start, count)
        first = (i * BLK + start) // HALF
        for k in range(first, first + count // HALF):
            tok_f[k, 0].wait_recv()
            if k < 7:
                tok_f[k, 1].wait_recv()
        far_tiles(i * BLK + start, count, 2, 6)
        for f in range(2):
            s1[f][0, 0, i, part, :256] = acc[2 + f, rows, :].astype(BF16)
            s1[f][0, 0, i, part, 256:] = acc[4 + f, rows, :].astype(BF16)
        for f in range(2):
            own, a = s1[f].at[0, 0, i, part], axes[f]
            for n, (k, d) in enumerate(((2, 2), (1, 3), (-1, 1))):
                ag[f, p, d] = remote(own, s1[f].at[0, d, i, part], ag_s.at[f, p, n], ag_r.at[f, p, n], ring(a, k))
            ag[f, p, "own"] = remote(own, s1[f].at[1, 0, i, part], ag_s.at[f, p, 3], ag_r.at[f, p, 3], sibling)

    def finish_query(i):
        rows = pl.ds(i * BLK, BLK)
        far_tiles(i * BLK, BLK, 0, 2)
        for f in range(2):
            qs[f, i] = acc[f, rows, :].astype(BF16)

    def to_sibling(p):
        i, start, count = pieces[p]
        part = pl.ds(start, count)
        for n, d in ((2, 2), (0, 3), (1, 1)):
            for f in range(2):
                ag[f, p, d].wait_recv()
                src, dst = s1[f].at[0, d, i, part], s1[f].at[1, d, i, part]
                ag[f, p, "s", d] = remote(src, dst, ag_s.at[f, p, 4 + n], ag_r.at[f, p, 4 + n], sibling)

    for copy in ids_x:
        copy.wait_recv()
    row = row + idg[0, 0] + idg[0, 1] + idg[0, 2]
    ids_z = spread(1, row, [(k, ring("z", k)) for k in (1, 2, 3)])

    for copy in wo_y:
        copy.wait_recv()
    left_cols, right_cols = pl.ds(0, 512), pl.ds(512, 512)
    three = pl.ds(1, 3)
    wo_1 = []
    for k in (2, 1, 3):
        own = wov.at[three, x, z, c, :, left_cols]
        wo_1.append(remote(own, own, wo_s.at[2 + k], wo_r.at[2 + k], ring("x", k)))
        own = wov.at[three, x, z, c, :, right_cols]
        wo_1.append(remote(own, own, wo_s.at[5 + k], wo_r.at[5 + k], ring("z", k)))

    tokens_event(0)
    for copy in w_local[3:]:
        copy.wait()
    for copy in ids_z:
        copy.wait_recv()
    row = row + idg[1, 0] + idg[1, 1] + idg[1, 2]
    ids_c = spread(2, row, [(1, sibling)])
    tokens_event(1)

    for copy in wo_1:
        copy.wait_recv()
    wo_2 = []
    for k in (2, 1, 3):
        own = wov.at[three, :, z, c, :, left_cols]
        wo_2.append(remote(own, own, wo_s.at[8 + k], wo_r.at[8 + k], ring("z", k)))
        own = wov.at[three, x, :, c, :, right_cols]
        wo_2.append(remote(own, own, wo_s.at[11 + k], wo_r.at[11 + k], ring("x", k)))

    near_tiles(0)
    ids_c[0].wait_recv()
    row = row + idg[2, 0]

    across = jnp.broadcast_to(row[0:1, :], (128, 128))
    down = across.T
    one = lax.broadcasted_iota(jnp.int32, (128, 128), 0)
    two = lax.broadcasted_iota(jnp.int32, (128, 128), 1)
    same = (across == down) & (one != two)
    partner = jnp.sum(jnp.where(same, one + 1, 0), axis=0, keepdims=True) - 1
    part_v[...] = jnp.broadcast_to(partner, (8, 128))
    part_copy = pltpu.make_async_copy(part_v, part_s, loc_sem.at[2])
    part_copy.start()

    tokens_event(2)
    finish_keys(0)
    tokens_event(3)
    finish_query(0)
    near_tiles(1)
    tokens_event(4)
    finish_keys(1)
    for copy in wo_2:
        copy.wait_recv()
    own = wov.at[three, :, :, c]
    wo_3 = remote(own, own, wo_s.at[15], wo_r.at[15], sibling)
    tokens_event(5)
    near_tiles(2)
    finish_keys(2)
    to_sibling(0)
    tokens_event(6)
    finish_query(1)
    finish_keys(3)
    tokens_event(7)
    near_tiles(3)
    finish_keys(4)
    finish_keys(5)
    to_sibling(1)
    to_sibling(2)
    finish_query(2)
    to_sibling(3)
    finish_query(3)
    part_copy.wait()
    to_sibling(4)
    to_sibling(5)

    def choice(f, k, i):
        dest = place(x, wrap(z + k), c) if f == 0 else place(wrap(x + k), z, c)
        p = part_s[0, dest * NB + i]
        at = jnp.maximum(p, 0)
        xp, zp = at // 32, lax.rem(at // 8, 4)
        cp, ip = lax.rem(at // 4, 2), lax.rem(at, 4)
        along, held = (xp - x, zp) if f == 0 else (zp - z, xp)
        return (lax.rem(cp + c, 2), wrap(along), ip), held, p

    second = ("z", "x")
    here = (z, x)
    for f in range(2):
        for p in range(len(pieces)):
            ag[f, p, "own"].wait_recv()
            for d in (1, 2, 3):
                ag[f, p, "s", d].wait_recv()

    low, high = pl.ds(0, HALF), pl.ds(HALF, HALF)
    rs = {}

    def pass_on(f, i, g, k, rows, to, dst, relay=None):
        index, held, _ = choice(f, k, i)
        packet = s1[f][index[0], index[1], index[2], rows]
        if relay is not None:
            packet = jnp.where(held == here[f], packet, rel[f, i, relay])
        tx[f, i, g] = packet
        rs[f, i, g] = remote(tx.at[f, i, g], dst, rs_s.at[f, i, g], rs_r.at[f, i, g], ring(second[f], to))

    def relay_out(i):
        for f in range(2):
            pass_on(f, i, 0, 2, low, 1, rel.at[f, i, 0])
            pass_on(f, i, 1, 2, high, -1, rel.at[f, i, 1])

    def direct_out(i):
        for f in range(2):
            pass_on(f, i, 2, 1, high, 1, fin.at[f, 0, i, high])
            pass_on(f, i, 3, -1, low, -1, fin.at[f, 1, i, low])

    def merged_out(i):
        for f in range(2):
            rs[f, i, 0].wait_recv()
            pass_on(f, i, 4, 1, low, 1, fin.at[f, 0, i, low], 0)
            rs[f, i, 1].wait_recv()
            pass_on(f, i, 5, -1, high, -1, fin.at[f, 1, i, high], 1)

    def attend(i, halves=(0, 1)):
        rows = pl.ds(i * BLK, BLK)
        for f in halves:
            for g in (2, 3, 4, 5):
                rs[f, i, g].wait_recv()
        for f in halves:
            index, held, p = choice(f, 0, i)
            at_left, at_right = held == wrap(here[f] - 1), held == wrap(here[f] + 1)
            for half, from_left in ((low, jnp.logical_not(at_right)), (high, at_left)):
                packet = jnp.where(from_left, fin[f, 0, i, half], fin[f, 1, i, half])
                own = s1[f][index[0], index[1], index[2], half]
                kvp[f, half] = jnp.where(held == here[f], own, packet)
            for j in range(2):
                kc, vc = pl.ds(j * HDIM, HDIM), pl.ds(256 + j * HDIM, HDIM)
                query = qs[f, i, :, kc]
                dims = (((1,), (1,)), ((), ()))
                near = lax.dot_general(query, s1[f][0, 0, i, :, kc], dims, preferred_element_type=F32) * SCALE
                far = lax.dot_general(query, kvp[f, :, kc], dims, preferred_element_type=F32) * SCALE
                far = jnp.where(p >= 0, far, -1e30)
                top = jnp.maximum(jnp.max(near, axis=1, keepdims=True), jnp.max(far, axis=1, keepdims=True))
                near, far = jnp.exp(near - top), jnp.exp(far - top)
                total = jnp.sum(near, axis=1, keepdims=True) + jnp.sum(far, axis=1, keepdims=True)
                near, far = (near / total).astype(BF16), (far / total).astype(BF16)
                mixed = jnp.dot(near, s1[f][0, 0, i, :, vc], preferred_element_type=F32)
                mixed += jnp.dot(far, kvp[f, :, vc], preferred_element_type=F32)
                mx[0, rows, pl.ds((2 * f + j) * HDIM, HDIM)] = mixed.astype(BF16)

    mx_c = {}

    def send_mixed(i):
        rows = pl.ds(i * BLK, BLK)
        mx_c[i, 0] = remote(mx.at[0, rows], mx.at[3, rows], mx_s.at[i, 0], mx_r.at[i, 0], ring("y", 1))
        mx_c[i, 1] = remote(mx.at[0, rows], mx.at[1, rows], mx_s.at[i, 1], mx_r.at[i, 1], ring("y", -1))

    def send_last(f):
        part = (pl.ds((NB - 1) * BLK, BLK), pl.ds(f * 256, 256))
        for n, (k, d) in enumerate(((2, 2), (1, 3), (-1, 1))):
            at = NB - 1 + f, n
            mx_c["last", f, d] = remote(mx.at[(0, *part)], mx.at[(d, *part)], mx_s.at[at], mx_r.at[at], ring("y", k))

    def forward_mixed(i):
        lo, hi = pl.ds(i * BLK, HALF), pl.ds(i * BLK + HALF, HALF)
        mx_c[i, 0].wait_recv()
        mx_c[i, 2] = remote(mx.at[3, lo], mx.at[2, lo], mx_s.at[i, 2], mx_r.at[i, 2], ring("y", 1))
        mx_c[i, 1].wait_recv()
        mx_c[i, 3] = remote(mx.at[1, hi], mx.at[2, hi], mx_s.at[i, 3], mx_r.at[i, 3], ring("y", -1))

    def project(i):
        rows = pl.ds(i * BLK, BLK)
        for n in (2, 3):
            mx_c[i, n].wait_recv()

        def tile(n, carry):
            cols = pl.ds(pl.multiple_of(n * 256, 256), 256)
            total = jnp.dot(mx[0, rows, :], wov[0, :, :, :, :, cols].reshape(WIDTH, 256), preferred_element_type=F32)
            for d in (1, 2, 3):
                part = wov[d, :, :, :, :, cols].reshape(WIDTH, 256)
                total += jnp.dot(mx[d, rows, :], part, preferred_element_type=F32)
            out[rows, cols] = total.astype(BF16)
            return carry

        lax.fori_loop(0, 4, tile, 0)

    def project_last(steps, store):
        rows = pl.ds((NB - 1) * BLK, BLK)

        def tile(n, carry):
            cols = pl.ds(pl.multiple_of(n * 256, 256), 256)
            total = jnp.zeros((BLK, 256), F32) if 0 in steps else acc[n, pl.ds(0, BLK), :]
            for d in steps:
                part = wov[d, :, :, :, :, cols].reshape(WIDTH, 256)
                total += jnp.dot(mx[d, rows, :], part, preferred_element_type=F32)
            if store:
                out[rows, cols] = total.astype(BF16)
            else:
                acc[n, pl.ds(0, BLK), :] = total
            return carry

        for d in steps:
            for f in range(2) if d else ():
                mx_c["last", f, d].wait_recv()
        lax.fori_loop(0, 4, tile, 0)

    before_exchange = len(started)
    relay_out(0)
    direct_out(0)
    relay_out(1)
    merged_out(0)
    direct_out(1)
    relay_out(2)
    merged_out(1)
    direct_out(2)
    relay_out(3)
    attend(0)
    send_mixed(0)
    merged_out(2)
    direct_out(3)
    attend(1)
    send_mixed(1)
    merged_out(3)
    forward_mixed(0)
    attend(2)
    send_mixed(2)
    forward_mixed(1)
    attend(3, (0,))
    send_last(0)
    attend(3, (1,))
    send_last(1)
    forward_mixed(2)
    wo_local.wait()
    wo_3.wait_recv()
    for copy in started[:before_exchange]:
        copy.wait_send()
    project(0)
    for copy in rs.values():
        copy.wait_send()
    project(1)
    project_last((0,), False)
    project(2)
    project_last((2,), False)
    project_last((3, 1), True)
    for copy in mx_c.values():
        copy.wait_send()


def per_device(tokens, w_query, w_key, w_value, w_out, block_bucket):
    anywhere = pl.BlockSpec(memory_space=pl.ANY)
    dma = pltpu.SemaphoreType.DMA
    return pl.pallas_call(
        kernel,
        out_shape=jax.ShapeDtypeStruct((NB * BLK, FEAT), BF16),
        in_specs=[pl.BlockSpec(memory_space=pltpu.SMEM)] + [anywhere] * 5,
        out_specs=pl.BlockSpec(memory_space=pltpu.VMEM),
        scratch_shapes=[
            pltpu.VMEM((4, NB * BLK, FEAT), BF16),
            pltpu.VMEM((4, 3, FEAT, WIDTH), BF16),
            pltpu.VMEM((6, NB * BLK, 256), F32),
            pltpu.VMEM((2, NB, BLK, 256), BF16),
            pltpu.VMEM((2, 4, NB, BLK, PACK), BF16),
            pltpu.VMEM((2, 4, NB, BLK, PACK), BF16),
            pltpu.VMEM((2, NB, 6, HALF, PACK), BF16),
            pltpu.VMEM((2, NB, 2, HALF, PACK), BF16),
            pltpu.VMEM((2, 2, NB, BLK, PACK), BF16),
            pltpu.VMEM((2, BLK, PACK), BF16),
            pltpu.VMEM((4, 4, 4, 2, 16, FEAT), BF16),
            pltpu.VMEM((4, NB * BLK, WIDTH), BF16),
            pltpu.VMEM((3, 3, 8, 128), jnp.int32),
            pltpu.VMEM((3, 8, 128), jnp.int32),
            pltpu.VMEM((8, 128), jnp.int32),
            pltpu.SMEM((8, 128), jnp.int32),
            dma((3,)),
            dma((4, 3)),
            dma((2 * NB, 4)),
            dma((2 * NB, 4)),
            dma((3, 3)),
            dma((3, 3)),
            dma((2, NB + 2, 7)),
            dma((2, NB + 2, 7)),
            dma((2, NB, 6)),
            dma((2, NB, 6)),
            dma((16,)),
            dma((16,)),
            dma((NB + 1, 4)),
            dma((NB + 1, 4)),
        ],
        compiler_params=pltpu.CompilerParams(
            collective_id=0, has_side_effects=True, vmem_limit_bytes=58 * 2**20
        ),
    )(block_bucket, tokens, w_query, w_key, w_value, w_out)


def solution(mesh):
    placed = (
        P("seq", "head"),
        P(None, "head"),
        P(None, "head"),
        P(None, "head"),
        P("head", None),
        P("seq"),
    )
    return jax.shard_map(
        per_device, mesh=mesh, in_specs=placed, out_specs=P("seq", "head"), check_vma=False
    )
```

```python
import jax
import jax.numpy as jnp
from jax import lax
from jax.experimental import pallas as pl
from jax.experimental.pallas import tpu as pltpu
from jax.sharding import PartitionSpec as P

HDIM = 128
SCALE = HDIM ** (-0.5)
BLK = 128
HALF = BLK // 2
NB = 4
FEAT = 1024
WIDTH = 512
PACK = 512
MESH = pl.DeviceIdType.MESH
F32 = jnp.float32
BF16 = jnp.bfloat16


def wrap(n):
    return lax.rem(n + 4, 4)


def kernel(
    ids, tok, wq, wk, wv, wo, out,
    tk, w, acc, qs, s1a, s1b, tx, rel, fin, kvp, wov, mx,
    idg, idsend, part_v, part_s,
    loc_sem, wloc_sem, tok_s, tok_r, id_s, id_r, ag_s, ag_r, rs_s, rs_r, wo_s, wo_r, mx_s, mx_r,
):
    s = lax.axis_index("seq")
    y = lax.axis_index("head")
    x = s // 8
    z = lax.rem(s // 2, 4)
    c = lax.rem(s, 2)
    s1 = (s1a, s1b)
    wo6 = wo.reshape(4, 4, 2, 16, 4 * FEAT)
    started = []

    def place(px, pz, pc):
        return (px * 4 + pz) * 2 + pc

    def ring(axis, k):
        if axis == "y":
            return (s, wrap(y + k))
        if axis == "x":
            return (place(wrap(x + k), z, c), y)
        return (place(x, wrap(z + k), c), y)

    sibling = (place(x, z, 1 - c), y)
    peers = [sibling] + [ring(a, k) for a in ("y", "x", "z") for k in (1, 2, 3)]

    def remote(src, dst, send, recv, device):
        copy = pltpu.make_async_remote_copy(
            src_ref=src, dst_ref=dst, send_sem=send, recv_sem=recv,
            device_id=device, device_id_type=MESH,
        )
        copy.start()
        started.append(copy)
        return copy

    barrier = pltpu.get_barrier_semaphore()
    for peer in peers:
        pl.semaphore_signal(barrier, inc=1, device_id=peer, device_id_type=MESH)

    tok_local = pltpu.make_async_copy(tok, tk.at[0], loc_sem.at[0])
    tok_local.start()
    w_local = []
    for d in (0, 3, 1, 2):
        rows = pl.ds(pl.multiple_of(wrap(y + d) * FEAT, FEAT), FEAT)
        for j, ref in enumerate((wq, wk, wv)):
            copy = pltpu.make_async_copy(ref.at[rows, :], w.at[d, j], wloc_sem.at[d, j])
            copy.start()
            w_local.append(copy)
    mine = pl.ds(pl.multiple_of(y * FEAT, FEAT), FEAT)
    wo_local = pltpu.make_async_copy(wo6.at[:, :, :, :, mine], wov.at[0], loc_sem.at[1])
    wo_local.start()

    pl.semaphore_wait(barrier, len(peers))

    wo_y = []
    row16 = pl.ds(pl.multiple_of(s * 16, 16), 16)
    for k in (1, 2, 3):
        cols = pl.ds(pl.multiple_of(wrap(y + k) * FEAT, FEAT), FEAT)
        wo_y.append(remote(wo.at[row16, cols], wov.at[4 - k, x, z, c], wo_s.at[k - 1], wo_r.at[k - 1], ring("y", k)))

    tok_c = {}
    tok_f = {}

    def send_tokens(k):
        rows = pl.ds(k * HALF, HALF)
        tok_c[k, 0] = remote(tok.at[rows, :], tk.at[3, rows, :], tok_s.at[k, 0], tok_r.at[k, 0], ring("y", 1))
        tok_c[k, 1] = remote(tok.at[rows, :], tk.at[1, rows, :], tok_s.at[k, 1], tok_r.at[k, 1], ring("y", -1))

    def tokens_event(k):
        lo, hi = pl.ds(k * HALF, HALF // 2), pl.ds(k * HALF + HALF // 2, HALF // 2)
        tok_c[k, 0].wait_recv()
        if k < 7:
            tok_f[k, 0] = remote(tk.at[3, lo, :], tk.at[2, lo, :], tok_s.at[k, 2], tok_r.at[k, 2], ring("y", 1))
        tok_c[k, 1].wait_recv()
        if k < 7:
            tok_f[k, 1] = remote(tk.at[1, hi, :], tk.at[2, hi, :], tok_s.at[k, 3], tok_r.at[k, 3], ring("y", -1))
        if k + 2 < 8:
            send_tokens(k + 2)
        if k == 6:
            rows = pl.ds(7 * HALF, HALF)
            tok_f[7, 0] = remote(tok.at[rows, :], tk.at[2, rows, :], tok_s.at[7, 2], tok_r.at[7, 2], ring("y", 2))

    send_tokens(0)
    send_tokens(1)

    lane = lax.broadcasted_iota(jnp.int32, (8, 128), 1)
    row = jnp.zeros((8, 128), jnp.int32)
    for i in range(NB):
        row = jnp.where(lane == s * NB + i, ids[i], row)

    def spread(stage, row, targets):
        idsend[stage] = row
        copies = []
        for k, target in targets:
            copies.append(
                remote(idsend.at[stage], idg.at[stage, k - 1], id_s.at[stage, k - 1], id_r.at[stage, k - 1], target)
            )
        return copies

    ids_x = spread(0, row, [(k, ring("x", k)) for k in (1, 2, 3)])

    tok_local.wait()
    for copy in w_local[:3]:
        copy.wait()

    def own_tile(t, carry):
        n, m = t // 2, lax.rem(t, 2)
        rows = pl.ds(pl.multiple_of(m * 256, 256), 256)
        cols = pl.ds(pl.multiple_of(lax.rem(n, 2) * 256, 256), 256)
        acc[n, rows, :] = jnp.dot(tk[0, rows, :], w[0, n // 2, :, cols], preferred_element_type=F32)
        return carry

    lax.fori_loop(0, 12, own_tile, 0)

    def near_tiles(i):
        rows = pl.ds(i * BLK, BLK)

        def tile(n, carry):
            cols = pl.ds(pl.multiple_of(lax.rem(n, 2) * 256, 256), 256)
            acc[n, rows, :] += jnp.dot(
                tk[3, rows, :], w[3, n // 2, :, cols], preferred_element_type=F32
            ) + jnp.dot(tk[1, rows, :], w[1, n // 2, :, cols], preferred_element_type=F32)
            return carry

        lax.fori_loop(0, 6, tile, 0)

    pieces = ((0, 0, BLK), (1, 0, BLK), (2, 0, HALF), (2, HALF, HALF), (3, 0, HALF), (3, HALF, HALF))

    def far_tiles(start, count, first, last):
        rows = pl.ds(start, count)

        def tile(n, carry):
            cols = pl.ds(pl.multiple_of(lax.rem(n, 2) * 256, 256), 256)
            acc[n, rows, :] += jnp.dot(tk[2, rows, :], w[2, n // 2, :, cols], preferred_element_type=F32)
            return carry

        lax.fori_loop(first, last, tile, 0)

    ag = {}
    axes = ("x", "z")

    def finish_keys(p):
        i, start, count = pieces[p]
        rows, part = pl.ds(i * BLK + start, count), pl.ds(start, count)
        first = (i * BLK + start) // HALF
        for k in range(first, first + count // HALF):
            tok_f[k, 0].wait_recv()
            if k < 7:
                tok_f[k, 1].wait_recv()
        far_tiles(i * BLK + start, count, 2, 6)
        for f in range(2):
            s1[f][0, 0, i, part, :256] = acc[2 + f, rows, :].astype(BF16)
            s1[f][0, 0, i, part, 256:] = acc[4 + f, rows, :].astype(BF16)
        for f in range(2):
            own, a = s1[f].at[0, 0, i, part], axes[f]
            for n, (k, d) in enumerate(((2, 2), (1, 3), (-1, 1))):
                ag[f, p, d] = remote(own, s1[f].at[0, d, i, part], ag_s.at[f, p, n], ag_r.at[f, p, n], ring(a, k))
            ag[f, p, "own"] = remote(own, s1[f].at[1, 0, i, part], ag_s.at[f, p, 3], ag_r.at[f, p, 3], sibling)

    def finish_query(i):
        rows = pl.ds(i * BLK, BLK)
        far_tiles(i * BLK, BLK, 0, 2)
        for f in range(2):
            qs[f, i] = acc[f, rows, :].astype(BF16)

    def to_sibling(p):
        i, start, count = pieces[p]
        part = pl.ds(start, count)
        for n, d in ((2, 2), (0, 3), (1, 1)):
            for f in range(2):
                ag[f, p, d].wait_recv()
                src, dst = s1[f].at[0, d, i, part], s1[f].at[1, d, i, part]
                ag[f, p, "s", d] = remote(src, dst, ag_s.at[f, p, 4 + n], ag_r.at[f, p, 4 + n], sibling)

    for copy in ids_x:
        copy.wait_recv()
    row = row + idg[0, 0] + idg[0, 1] + idg[0, 2]
    ids_z = spread(1, row, [(k, ring("z", k)) for k in (1, 2, 3)])

    for copy in wo_y:
        copy.wait_recv()
    left_cols, right_cols = pl.ds(0, 512), pl.ds(512, 512)
    three = pl.ds(1, 3)
    wo_1 = []
    for k in (2, 1, 3):
        own = wov.at[three, x, z, c, :, left_cols]
        wo_1.append(remote(own, own, wo_s.at[2 + k], wo_r.at[2 + k], ring("x", k)))
        own = wov.at[three, x, z, c, :, right_cols]
        wo_1.append(remote(own, own, wo_s.at[5 + k], wo_r.at[5 + k], ring("z", k)))

    tokens_event(0)
    for copy in w_local[3:]:
        copy.wait()
    for copy in ids_z:
        copy.wait_recv()
    row = row + idg[1, 0] + idg[1, 1] + idg[1, 2]
    ids_c = spread(2, row, [(1, sibling)])
    tokens_event(1)

    for copy in wo_1:
        copy.wait_recv()
    wo_2 = []
    for k in (2, 1, 3):
        own = wov.at[three, :, z, c, :, left_cols]
        wo_2.append(remote(own, own, wo_s.at[8 + k], wo_r.at[8 + k], ring("z", k)))
        own = wov.at[three, x, :, c, :, right_cols]
        wo_2.append(remote(own, own, wo_s.at[11 + k], wo_r.at[11 + k], ring("x", k)))

    near_tiles(0)
    ids_c[0].wait_recv()
    row = row + idg[2, 0]

    across = jnp.broadcast_to(row[0:1, :], (128, 128))
    down = across.T
    one = lax.broadcasted_iota(jnp.int32, (128, 128), 0)
    two = lax.broadcasted_iota(jnp.int32, (128, 128), 1)
    same = (across == down) & (one != two)
    partner = jnp.sum(jnp.where(same, one + 1, 0), axis=0, keepdims=True) - 1
    part_v[...] = jnp.broadcast_to(partner, (8, 128))
    part_copy = pltpu.make_async_copy(part_v, part_s, loc_sem.at[2])
    part_copy.start()

    tokens_event(2)
    finish_keys(0)
    tokens_event(3)
    finish_query(0)
    near_tiles(1)
    tokens_event(4)
    finish_keys(1)
    for copy in wo_2:
        copy.wait_recv()
    own = wov.at[three, :, :, c]
    wo_3 = remote(own, own, wo_s.at[15], wo_r.at[15], sibling)
    tokens_event(5)
    near_tiles(2)
    finish_keys(2)
    to_sibling(0)
    tokens_event(6)
    finish_query(1)
    finish_keys(3)
    tokens_event(7)
    near_tiles(3)
    finish_keys(4)
    finish_keys(5)
    to_sibling(1)
    to_sibling(2)
    finish_query(2)
    to_sibling(3)
    finish_query(3)
    part_copy.wait()
    to_sibling(4)
    to_sibling(5)

    def choice(f, k, i):
        dest = place(x, wrap(z + k), c) if f == 0 else place(wrap(x + k), z, c)
        p = part_s[0, dest * NB + i]
        at = jnp.maximum(p, 0)
        xp, zp = at // 32, lax.rem(at // 8, 4)
        cp, ip = lax.rem(at // 4, 2), lax.rem(at, 4)
        along, held = (xp - x, zp) if f == 0 else (zp - z, xp)
        return (lax.rem(cp + c, 2), wrap(along), ip), held, p

    second = ("z", "x")
    here = (z, x)
    for f in range(2):
        for p in range(len(pieces)):
            ag[f, p, "own"].wait_recv()
            for d in (1, 2, 3):
                ag[f, p, "s", d].wait_recv()

    low, high = pl.ds(0, HALF), pl.ds(HALF, HALF)
    rs = {}

    def pass_on(f, i, g, k, rows, to, dst, relay=None):
        index, held, _ = choice(f, k, i)
        packet = s1[f][index[0], index[1], index[2], rows]
        if relay is not None:
            packet = jnp.where(held == here[f], packet, rel[f, i, relay])
        tx[f, i, g] = packet
        rs[f, i, g] = remote(tx.at[f, i, g], dst, rs_s.at[f, i, g], rs_r.at[f, i, g], ring(second[f], to))

    def relay_out(i):
        for f in range(2):
            pass_on(f, i, 0, 2, low, 1, rel.at[f, i, 0])
            pass_on(f, i, 1, 2, high, -1, rel.at[f, i, 1])

    def direct_out(i):
        for f in range(2):
            pass_on(f, i, 2, 1, high, 1, fin.at[f, 0, i, high])
            pass_on(f, i, 3, -1, low, -1, fin.at[f, 1, i, low])

    def merged_out(i):
        for f in range(2):
            rs[f, i, 0].wait_recv()
            pass_on(f, i, 4, 1, low, 1, fin.at[f, 0, i, low], 0)
            rs[f, i, 1].wait_recv()
            pass_on(f, i, 5, -1, high, -1, fin.at[f, 1, i, high], 1)

    def attend(i, halves=(0, 1)):
        rows = pl.ds(i * BLK, BLK)
        for f in halves:
            for g in (2, 3, 4, 5):
                rs[f, i, g].wait_recv()
        for f in halves:
            index, held, p = choice(f, 0, i)
            at_left, at_right = held == wrap(here[f] - 1), held == wrap(here[f] + 1)
            for half, from_left in ((low, jnp.logical_not(at_right)), (high, at_left)):
                packet = jnp.where(from_left, fin[f, 0, i, half], fin[f, 1, i, half])
                own = s1[f][index[0], index[1], index[2], half]
                kvp[f, half] = jnp.where(held == here[f], own, packet)
            for j in range(2):
                kc, vc = pl.ds(j * HDIM, HDIM), pl.ds(256 + j * HDIM, HDIM)
                query = qs[f, i, :, kc]
                dims = (((1,), (1,)), ((), ()))
                near = lax.dot_general(query, s1[f][0, 0, i, :, kc], dims, preferred_element_type=F32) * SCALE
                far = lax.dot_general(query, kvp[f, :, kc], dims, preferred_element_type=F32) * SCALE
                far = jnp.where(p >= 0, far, -1e30)
                top = jnp.maximum(jnp.max(near, axis=1, keepdims=True), jnp.max(far, axis=1, keepdims=True))
                near, far = jnp.exp(near - top), jnp.exp(far - top)
                total = jnp.sum(near, axis=1, keepdims=True) + jnp.sum(far, axis=1, keepdims=True)
                near, far = (near / total).astype(BF16), (far / total).astype(BF16)
                mixed = jnp.dot(near, s1[f][0, 0, i, :, vc], preferred_element_type=F32)
                mixed += jnp.dot(far, kvp[f, :, vc], preferred_element_type=F32)
                mx[0, rows, pl.ds((2 * f + j) * HDIM, HDIM)] = mixed.astype(BF16)

    mx_c = {}

    def send_mixed(i):
        rows = pl.ds(i * BLK, BLK)
        mx_c[i, 0] = remote(mx.at[0, rows], mx.at[3, rows], mx_s.at[i, 0], mx_r.at[i, 0], ring("y", 1))
        mx_c[i, 1] = remote(mx.at[0, rows], mx.at[1, rows], mx_s.at[i, 1], mx_r.at[i, 1], ring("y", -1))

    def send_last(f):
        part = (pl.ds((NB - 1) * BLK, BLK), pl.ds(f * 256, 256))
        for n, (k, d) in enumerate(((2, 2), (1, 3), (-1, 1))):
            at = NB - 1 + f, n
            mx_c["last", f, d] = remote(mx.at[(0, *part)], mx.at[(d, *part)], mx_s.at[at], mx_r.at[at], ring("y", k))

    def forward_mixed(i):
        lo, hi = pl.ds(i * BLK, HALF), pl.ds(i * BLK + HALF, HALF)
        mx_c[i, 0].wait_recv()
        mx_c[i, 2] = remote(mx.at[3, lo], mx.at[2, lo], mx_s.at[i, 2], mx_r.at[i, 2], ring("y", 1))
        mx_c[i, 1].wait_recv()
        mx_c[i, 3] = remote(mx.at[1, hi], mx.at[2, hi], mx_s.at[i, 3], mx_r.at[i, 3], ring("y", -1))

    def project(i):
        rows = pl.ds(i * BLK, BLK)
        for n in (2, 3):
            mx_c[i, n].wait_recv()

        def tile(n, carry):
            cols = pl.ds(pl.multiple_of(n * 256, 256), 256)
            total = jnp.dot(mx[0, rows, :], wov[0, :, :, :, :, cols].reshape(WIDTH, 256), preferred_element_type=F32)
            for d in (1, 2, 3):
                part = wov[d, :, :, :, :, cols].reshape(WIDTH, 256)
                total += jnp.dot(mx[d, rows, :], part, preferred_element_type=F32)
            out[rows, cols] = total.astype(BF16)
            return carry

        lax.fori_loop(0, 4, tile, 0)

    def project_last(steps, store):
        rows = pl.ds((NB - 1) * BLK, BLK)

        def tile(n, carry):
            cols = pl.ds(pl.multiple_of(n * 256, 256), 256)
            total = jnp.zeros((BLK, 256), F32) if 0 in steps else acc[n, pl.ds(0, BLK), :]
            for d in steps:
                part = wov[d, :, :, :, :, cols].reshape(WIDTH, 256)
                total += jnp.dot(mx[d, rows, :], part, preferred_element_type=F32)
            if store:
                out[rows, cols] = total.astype(BF16)
            else:
                acc[n, pl.ds(0, BLK), :] = total
            return carry

        for d in steps:
            for f in range(2) if d else ():
                mx_c["last", f, d].wait_recv()
        lax.fori_loop(0, 4, tile, 0)

    before_exchange = len(started)
    relay_out(0)
    direct_out(0)
    relay_out(1)
    merged_out(0)
    direct_out(1)
    relay_out(2)
    merged_out(1)
    direct_out(2)
    relay_out(3)
    attend(0)
    send_mixed(0)
    merged_out(2)
    direct_out(3)
    attend(1)
    send_mixed(1)
    merged_out(3)
    forward_mixed(0)
    attend(2)
    send_mixed(2)
    forward_mixed(1)
    attend(3, (0,))
    send_last(0)
    attend(3, (1,))
    send_last(1)
    forward_mixed(2)
    wo_local.wait()
    wo_3.wait_recv()
    for copy in started[:before_exchange]:
        copy.wait_send()
    project(0)
    for copy in rs.values():
        copy.wait_send()
    project(1)
    project_last((0,), False)
    project(2)
    project_last((2,), False)
    project_last((3, 1), True)
    for copy in mx_c.values():
        copy.wait_send()


def per_device(tokens, w_query, w_key, w_value, w_out, block_bucket):
    anywhere = pl.BlockSpec(memory_space=pl.ANY)
    dma = pltpu.SemaphoreType.DMA
    return pl.pallas_call(
        kernel,
        out_shape=pltpu.VMEM((NB * BLK, FEAT), BF16),
        in_specs=[pl.BlockSpec(memory_space=pltpu.SMEM)] + [anywhere] * 5,
        out_specs=pl.BlockSpec(memory_space=pltpu.VMEM),
        scratch_shapes=[
            pltpu.VMEM((4, NB * BLK, FEAT), BF16),
            pltpu.VMEM((4, 3, FEAT, WIDTH), BF16),
            pltpu.VMEM((6, NB * BLK, 256), F32),
            pltpu.VMEM((2, NB, BLK, 256), BF16),
            pltpu.VMEM((2, 4, NB, BLK, PACK), BF16),
            pltpu.VMEM((2, 4, NB, BLK, PACK), BF16),
            pltpu.VMEM((2, NB, 6, HALF, PACK), BF16),
            pltpu.VMEM((2, NB, 2, HALF, PACK), BF16),
            pltpu.VMEM((2, 2, NB, BLK, PACK), BF16),
            pltpu.VMEM((2, BLK, PACK), BF16),
            pltpu.VMEM((4, 4, 4, 2, 16, FEAT), BF16),
            pltpu.VMEM((4, NB * BLK, WIDTH), BF16),
            pltpu.VMEM((3, 3, 8, 128), jnp.int32),
            pltpu.VMEM((3, 8, 128), jnp.int32),
            pltpu.VMEM((8, 128), jnp.int32),
            pltpu.SMEM((8, 128), jnp.int32),
            dma((3,)),
            dma((4, 3)),
            dma((2 * NB, 4)),
            dma((2 * NB, 4)),
            dma((3, 3)),
            dma((3, 3)),
            dma((2, NB + 2, 7)),
            dma((2, NB + 2, 7)),
            dma((2, NB, 6)),
            dma((2, NB, 6)),
            dma((16,)),
            dma((16,)),
            dma((NB + 1, 4)),
            dma((NB + 1, 4)),
        ],
        compiler_params=pltpu.CompilerParams(
            collective_id=0, has_side_effects=True, vmem_limit_bytes=58 * 2**20
        ),
    )(block_bucket, tokens, w_query, w_key, w_value, w_out)


def solution(mesh):
    placed = (
        P("seq", "head"),
        P(None, "head"),
        P(None, "head"),
        P(None, "head"),
        P("head", None),
        P("seq"),
    )
    return jax.shard_map(
        per_device, mesh=mesh, in_specs=placed, out_specs=P("seq", "head"), check_vma=False
    )
```

```python
import jax
import jax.numpy as jnp
from jax import lax
from jax.experimental import pallas as pl
from jax.experimental.pallas import tpu as pltpu
from jax.sharding import PartitionSpec as P

HDIM = 128
SCALE = HDIM ** (-0.5)
BLK = 128
HALF = BLK // 2
NB = 4
FEAT = 1024
WIDTH = 512
PACK = 512
UNIT = 256
MESH = pl.DeviceIdType.MESH
F32 = jnp.float32
BF16 = jnp.bfloat16


def wrap(n):
    return lax.rem(n + 4, 4)


def kernel(
    ids, tok, wq, wk, wv, wo, out,
    tk, w, acc, qs, s1a, s1b, tx, rel, fin, kvp, wov, mx,
    idg, idsend, part_v, part_s,
    loc_sem, wloc_sem, tok_s, tok_r, id_s, id_r, ag_s, ag_r, rs_s, rs_r, wo_s, wo_r, mx_s, mx_r,
):
    s = lax.axis_index("seq")
    y = lax.axis_index("head")
    x = s // 8
    z = lax.rem(s // 2, 4)
    c = lax.rem(s, 2)
    s1 = (s1a, s1b)
    px = lax.rem(x, 2) * 2 + x // 2
    wo6 = wo.reshape(4, 4, 2, 16, 4 * FEAT)
    started = []

    def place(px, pz, pc):
        return (px * 4 + pz) * 2 + pc

    def ring(axis, k):
        if axis == "y":
            return (s, wrap(y + k))
        if axis == "x":
            return (place(wrap(x + k), z, c), y)
        return (place(x, wrap(z + k), c), y)

    sibling = (place(x, z, 1 - c), y)
    peers = [sibling] + [ring(a, k) for a in ("y", "x", "z") for k in (1, 2, 3)]

    def remote(src, dst, send, recv, device):
        copy = pltpu.make_async_remote_copy(
            src_ref=src, dst_ref=dst, send_sem=send, recv_sem=recv,
            device_id=device, device_id_type=MESH,
        )
        copy.start()
        started.append(copy)
        return copy

    barrier = pltpu.get_barrier_semaphore()
    for peer in peers:
        pl.semaphore_signal(barrier, inc=1, device_id=peer, device_id_type=MESH)

    tok_local = pltpu.make_async_copy(tok, tk.at[0], loc_sem.at[0])
    tok_local.start()
    w_local = []
    for d in (0, 3, 1, 2):
        rows = pl.ds(pl.multiple_of(wrap(y + d) * FEAT, FEAT), FEAT)
        for j, ref in enumerate((wq, wk, wv)):
            copy = pltpu.make_async_copy(ref.at[rows, :], w.at[d, j], wloc_sem.at[d, j])
            copy.start()
            w_local.append(copy)
    mine = pl.ds(pl.multiple_of(y * FEAT, FEAT), FEAT)
    wo_local = []
    for h in range(4):
        src, dst = wo6.at[h, :, :, :, mine], wov.at[0, h % 2 * 2 + h // 2]
        wo_local.append(pltpu.make_async_copy(src, dst, loc_sem.at[3 + h]))
    for copy in wo_local:
        copy.start()

    pl.semaphore_wait(barrier, len(peers))

    wo_y = []
    row16 = pl.ds(pl.multiple_of(s * 16, 16), 16)
    for k in (1, 2, 3):
        cols = pl.ds(pl.multiple_of(wrap(y + k) * FEAT, FEAT), FEAT)
        wo_y.append(remote(wo.at[row16, cols], wov.at[4 - k, px, z, c], wo_s.at[k - 1], wo_r.at[k - 1], ring("y", k)))

    tok_c = {}
    tok_f = {}

    def send_tokens(k):
        rows = pl.ds(k * HALF, HALF)
        tok_c[k, 0] = remote(tok.at[rows, :], tk.at[3, rows, :], tok_s.at[k, 0], tok_r.at[k, 0], ring("y", 1))
        tok_c[k, 1] = remote(tok.at[rows, :], tk.at[1, rows, :], tok_s.at[k, 1], tok_r.at[k, 1], ring("y", -1))

    def tokens_event(k):
        lo, hi = pl.ds(k * HALF, HALF // 2), pl.ds(k * HALF + HALF // 2, HALF // 2)
        tok_c[k, 0].wait_recv()
        if k < 7:
            tok_f[k, 0] = remote(tk.at[3, lo, :], tk.at[2, lo, :], tok_s.at[k, 2], tok_r.at[k, 2], ring("y", 1))
        tok_c[k, 1].wait_recv()
        if k < 7:
            tok_f[k, 1] = remote(tk.at[1, hi, :], tk.at[2, hi, :], tok_s.at[k, 3], tok_r.at[k, 3], ring("y", -1))
        if k + 2 < 8:
            send_tokens(k + 2)
        if k == 6:
            rows = pl.ds(7 * HALF, HALF)
            tok_f[7, 0] = remote(tok.at[rows, :], tk.at[2, rows, :], tok_s.at[7, 2], tok_r.at[7, 2], ring("y", 2))

    send_tokens(0)
    send_tokens(1)

    lane = lax.broadcasted_iota(jnp.int32, (8, 128), 1)
    row = jnp.zeros((8, 128), jnp.int32)
    for i in range(NB):
        row = jnp.where(lane == s * NB + i, ids[i], row)

    def spread(stage, row, targets):
        idsend[stage] = row
        copies = []
        for k, target in targets:
            copies.append(
                remote(idsend.at[stage], idg.at[stage, k - 1], id_s.at[stage, k - 1], id_r.at[stage, k - 1], target)
            )
        return copies

    ids_x = spread(0, row, [(k, ring("x", k)) for k in (1, 2, 3)])

    tok_local.wait()
    for copy in w_local[:3]:
        copy.wait()

    def own_tile(t, carry):
        n, m = t // 2, lax.rem(t, 2)
        rows = pl.ds(pl.multiple_of(m * 256, 256), 256)
        cols = pl.ds(pl.multiple_of(lax.rem(n, 2) * 256, 256), 256)
        acc[n, rows, :] = jnp.dot(tk[0, rows, :], w[0, n // 2, :, cols], preferred_element_type=F32)
        return carry

    lax.fori_loop(0, 12, own_tile, 0)

    def near_tiles(i):
        rows = pl.ds(i * BLK, BLK)

        def tile(n, carry):
            cols = pl.ds(pl.multiple_of(lax.rem(n, 2) * 256, 256), 256)
            acc[n, rows, :] += jnp.dot(
                tk[3, rows, :], w[3, n // 2, :, cols], preferred_element_type=F32
            ) + jnp.dot(tk[1, rows, :], w[1, n // 2, :, cols], preferred_element_type=F32)
            return carry

        lax.fori_loop(0, 6, tile, 0)

    pieces = ((0, 0, BLK), (1, 0, BLK), (2, 0, HALF), (2, HALF, HALF), (3, 0, HALF), (3, HALF, HALF))

    def far_tiles(start, count, first, last):
        rows = pl.ds(start, count)

        def tile(n, carry):
            cols = pl.ds(pl.multiple_of(lax.rem(n, 2) * 256, 256), 256)
            acc[n, rows, :] += jnp.dot(tk[2, rows, :], w[2, n // 2, :, cols], preferred_element_type=F32)
            return carry

        lax.fori_loop(first, last, tile, 0)

    ag = {}
    axes = ("x", "z")

    def finish_keys(p):
        i, start, count = pieces[p]
        rows, part = pl.ds(i * BLK + start, count), pl.ds(start, count)
        first = (i * BLK + start) // HALF
        for k in range(first, first + count // HALF):
            tok_f[k, 0].wait_recv()
            if k < 7:
                tok_f[k, 1].wait_recv()
        far_tiles(i * BLK + start, count, 2, 6)
        for f in range(2):
            for j in range(2):
                head = pl.ds(j * HDIM, HDIM)
                s1[f][0, 0, i, part, pl.ds(j * 256, HDIM)] = acc[2 + f, rows, head].astype(BF16)
                s1[f][0, 0, i, part, pl.ds(j * 256 + HDIM, HDIM)] = acc[4 + f, rows, head].astype(BF16)
        for f in range(2):
            own, a = s1[f].at[0, 0, i, part], axes[f]
            for n, (k, d) in enumerate(((2, 2), (1, 3), (-1, 1))):
                ag[f, p, d] = remote(own, s1[f].at[0, d, i, part], ag_s.at[f, p, n], ag_r.at[f, p, n], ring(a, k))
            ag[f, p, "own"] = remote(own, s1[f].at[1, 0, i, part], ag_s.at[f, p, 3], ag_r.at[f, p, 3], sibling)

    def finish_query(i):
        rows = pl.ds(i * BLK, BLK)
        far_tiles(i * BLK, BLK, 0, 2)
        for f in range(2):
            qs[f, i] = acc[f, rows, :].astype(BF16)

    def to_sibling(p):
        i, start, count = pieces[p]
        part = pl.ds(start, count)
        for n, d in ((2, 2), (0, 3), (1, 1)):
            for f in range(2):
                ag[f, p, d].wait_recv()
                src, dst = s1[f].at[0, d, i, part], s1[f].at[1, d, i, part]
                ag[f, p, "s", d] = remote(src, dst, ag_s.at[f, p, 4 + n], ag_r.at[f, p, 4 + n], sibling)

    for copy in ids_x:
        copy.wait_recv()
    row = row + idg[0, 0] + idg[0, 1] + idg[0, 2]
    ids_z = spread(1, row, [(k, ring("z", k)) for k in (1, 2, 3)])

    for copy in wo_y:
        copy.wait_recv()
    left_cols, right_cols = pl.ds(0, 512), pl.ds(512, 512)
    three = pl.ds(1, 3)
    wo_1 = []
    for k in (2, 1, 3):
        own = wov.at[three, px, z, c, :, left_cols]
        wo_1.append(remote(own, own, wo_s.at[2 + k], wo_r.at[2 + k], ring("x", k)))
        own = wov.at[three, px, z, c, :, right_cols]
        wo_1.append(remote(own, own, wo_s.at[5 + k], wo_r.at[5 + k], ring("z", k)))

    tokens_event(0)
    for copy in w_local[3:]:
        copy.wait()
    for copy in ids_z:
        copy.wait_recv()
    row = row + idg[1, 0] + idg[1, 1] + idg[1, 2]
    ids_c = spread(2, row, [(1, sibling)])
    tokens_event(1)

    for copy in wo_1:
        copy.wait_recv()
    wo_2 = []
    for k in (2, 1, 3):
        own = wov.at[three, :, z, c, :, left_cols]
        wo_2.append(remote(own, own, wo_s.at[8 + k], wo_r.at[8 + k], ring("z", k)))
        own = wov.at[three, px, :, c, :, right_cols]
        wo_2.append(remote(own, own, wo_s.at[11 + k], wo_r.at[11 + k], ring("x", k)))

    near_tiles(0)
    ids_c[0].wait_recv()
    row = row + idg[2, 0]

    across = jnp.broadcast_to(row[0:1, :], (128, 128))
    down = across.T
    one = lax.broadcasted_iota(jnp.int32, (128, 128), 0)
    two = lax.broadcasted_iota(jnp.int32, (128, 128), 1)
    same = (across == down) & (one != two)
    partner = jnp.sum(jnp.where(same, one + 1, 0), axis=0, keepdims=True) - 1
    part_v[...] = jnp.broadcast_to(partner, (8, 128))
    part_copy = pltpu.make_async_copy(part_v, part_s, loc_sem.at[2])
    part_copy.start()

    tokens_event(2)
    finish_keys(0)
    tokens_event(3)
    finish_query(0)
    near_tiles(1)
    tokens_event(4)
    finish_keys(1)
    for copy in wo_2:
        copy.wait_recv()
    own = wov.at[three, :, :, c]
    wo_3 = remote(own, own, wo_s.at[15], wo_r.at[15], sibling)
    tokens_event(5)
    near_tiles(2)
    finish_keys(2)
    to_sibling(0)
    tokens_event(6)
    finish_query(1)
    finish_keys(3)
    tokens_event(7)
    near_tiles(3)
    finish_keys(4)
    finish_keys(5)
    to_sibling(1)
    to_sibling(2)
    finish_query(2)
    to_sibling(3)
    finish_query(3)
    part_copy.wait()
    to_sibling(4)
    to_sibling(5)

    def choice(f, k, i):
        dest = place(x, wrap(z + k), c) if f == 0 else place(wrap(x + k), z, c)
        p = part_s[0, dest * NB + i]
        at = jnp.maximum(p, 0)
        xp, zp = at // 32, lax.rem(at // 8, 4)
        cp, ip = lax.rem(at // 4, 2), lax.rem(at, 4)
        along, held = (xp - x, zp) if f == 0 else (zp - z, xp)
        return (lax.rem(cp + c, 2), wrap(along), ip), held, p

    second = ("z", "x")
    here = (z, x)
    for f in range(2):
        for p in range(len(pieces)):
            ag[f, p, "own"].wait_recv()
            for d in (1, 2, 3):
                ag[f, p, "s", d].wait_recv()

    low, high = pl.ds(0, HALF), pl.ds(HALF, HALF)
    rs = {}
    choices = {}

    def chosen(f, k, i):
        if (f, k, i) not in choices:
            choices[f, k, i] = choice(f, k, i)
        return choices[f, k, i]

    def pass_on(f, u, g, k, rows, to, dst, relay=None):
        i, j = divmod(u, 2)
        index, held, _ = chosen(f, k, i)
        packet = s1[f][index[0], index[1], index[2], rows, pl.ds(j * UNIT, UNIT)]
        if relay is not None:
            packet = jnp.where(held == here[f], packet, rel[f, u, relay])
        tx[f, u, g] = packet
        rs[f, u, g] = remote(tx.at[f, u, g], dst, rs_s.at[f, u, g], rs_r.at[f, u, g], ring(second[f], to))

    def relay_out(u):
        for f in range(2):
            pass_on(f, u, 0, 2, low, 1, rel.at[f, u, 0])
            pass_on(f, u, 1, 2, high, -1, rel.at[f, u, 1])

    def direct_out(u):
        for f in range(2):
            pass_on(f, u, 2, 1, high, 1, fin.at[f, 0, u, high])
            pass_on(f, u, 3, -1, low, -1, fin.at[f, 1, u, low])

    def merged_out(u):
        for f in range(2):
            rs[f, u, 0].wait_recv()
            pass_on(f, u, 4, 1, low, 1, fin.at[f, 0, u, low], 0)
            rs[f, u, 1].wait_recv()
            pass_on(f, u, 5, -1, high, -1, fin.at[f, 1, u, high], 1)

    mx_c = {}

    def send_mixed(u):
        i, j = divmod(u, 2)
        rows = pl.ds(i * BLK, BLK)
        own = mx.at[0, j, rows]
        if u == 7:
            mx_c[u, 2] = remote(own, mx.at[2, j, rows], mx_s.at[u, 2], mx_r.at[u, 2], ring("y", 2))
        mx_c[u, 0] = remote(own, mx.at[3, j, rows], mx_s.at[u, 0], mx_r.at[u, 0], ring("y", 1))
        mx_c[u, 1] = remote(own, mx.at[1, j, rows], mx_s.at[u, 1], mx_r.at[u, 1], ring("y", -1))

    def forward_mixed(u):
        i, j = divmod(u, 2)
        lo, hi = pl.ds(i * BLK, HALF), pl.ds(i * BLK + HALF, HALF)
        mx_c[u, 0].wait_recv()
        mx_c[u, 2] = remote(mx.at[3, j, lo], mx.at[2, j, lo], mx_s.at[u, 2], mx_r.at[u, 2], ring("y", 1))
        mx_c[u, 1].wait_recv()
        mx_c[u, 3] = remote(mx.at[1, j, hi], mx.at[2, j, hi], mx_s.at[u, 3], mx_r.at[u, 3], ring("y", -1))

    def attend(u):
        i, j = divmod(u, 2)
        rows = pl.ds(i * BLK, BLK)
        for f in range(2):
            for g in (2, 3, 4, 5):
                rs[f, u, g].wait_recv()
        kc, vc = pl.ds(j * UNIT, HDIM), pl.ds(j * UNIT + HDIM, HDIM)
        for f in range(2):
            index, held, p = chosen(f, 0, i)
            at_left, at_right = held == wrap(here[f] - 1), held == wrap(here[f] + 1)
            for half, from_left in ((low, jnp.logical_not(at_right)), (high, at_left)):
                packet = jnp.where(from_left, fin[f, 0, u, half], fin[f, 1, u, half])
                own = s1[f][index[0], index[1], index[2], half, pl.ds(j * UNIT, UNIT)]
                kvp[f, half] = jnp.where(held == here[f], own, packet)
            query = qs[f, i, :, pl.ds(j * HDIM, HDIM)]
            dims = (((1,), (1,)), ((), ()))
            near = lax.dot_general(query, s1[f][0, 0, i, :, kc], dims, preferred_element_type=F32) * SCALE
            far = lax.dot_general(query, kvp[f, :, :HDIM], dims, preferred_element_type=F32) * SCALE
            far = jnp.where(p >= 0, far, -1e30)
            top = jnp.maximum(jnp.max(near, axis=1, keepdims=True), jnp.max(far, axis=1, keepdims=True))
            near, far = jnp.exp(near - top), jnp.exp(far - top)
            total = jnp.sum(near, axis=1, keepdims=True) + jnp.sum(far, axis=1, keepdims=True)
            near, far = (near / total).astype(BF16), (far / total).astype(BF16)
            mixed = jnp.dot(near, s1[f][0, 0, i, :, vc], preferred_element_type=F32)
            mixed += jnp.dot(far, kvp[f, :, HDIM:], preferred_element_type=F32)
            mx[0, j, rows, pl.ds(f * HDIM, HDIM)] = mixed.astype(BF16)
        send_mixed(u)

    def project(i, steps, first=True, last=True):
        rows = pl.ds(i * BLK, BLK)

        def tile(n, carry):
            cols = pl.ds(pl.multiple_of(n * 256, 256), 256)
            total = jnp.zeros((BLK, 256), F32) if first else acc[n, pl.ds(0, BLK), :]
            for d, j in steps:
                part = wov[d, pl.ds(2 * j, 2), :, :, :, cols].reshape(256, 256)
                total += jnp.dot(mx[d, j, rows, :], part, preferred_element_type=F32)
            if last:
                out[rows, cols] = total.astype(BF16)
            else:
                acc[n, pl.ds(0, BLK), :] = total
            return carry

        lax.fori_loop(0, 4, tile, 0)

    def arrived(*units):
        for u in units:
            for n in (0, 1, 2) if u == 7 else (2, 3):
                mx_c[u, n].wait_recv()

    before_exchange = len(started)
    for u in (0, 1, 2):
        relay_out(u)
        direct_out(u)
    merged_out(0)
    relay_out(3)
    direct_out(3)
    merged_out(1)
    relay_out(4)
    relay_out(5)
    merged_out(2)
    direct_out(4)
    relay_out(6)
    attend(0)
    merged_out(3)
    direct_out(5)
    relay_out(7)
    attend(1)
    merged_out(4)
    direct_out(6)
    merged_out(5)
    direct_out(7)
    attend(2)
    forward_mixed(0)
    merged_out(6)
    attend(3)
    forward_mixed(1)
    merged_out(7)
    attend(4)
    forward_mixed(2)
    attend(5)
    attend(6)
    forward_mixed(3)
    attend(7)
    forward_mixed(4)
    forward_mixed(5)
    for copy in wo_local:
        copy.wait()
    wo_3.wait_recv()
    every = [(d, j) for d in range(4) for j in range(2)]
    arrived(0, 1)
    project(0, every)
    forward_mixed(6)
    for copy in started[:before_exchange]:
        copy.wait_send()
    project(3, every[:2], True, False)
    arrived(2, 3)
    project(1, every)
    for copy in rs.values():
        copy.wait_send()
    arrived(4, 5)
    project(2, every)
    arrived(6)
    project(3, [(d, 0) for d in (1, 2, 3)], False, False)
    arrived(7)
    project(3, [(d, 1) for d in (1, 2, 3)], False, True)
    for copy in mx_c.values():
        copy.wait_send()


def per_device(tokens, w_query, w_key, w_value, w_out, block_bucket):
    anywhere = pl.BlockSpec(memory_space=pl.ANY)
    dma = pltpu.SemaphoreType.DMA
    return pl.pallas_call(
        kernel,
        out_shape=pltpu.VMEM((NB * BLK, FEAT), BF16),
        in_specs=[pl.BlockSpec(memory_space=pltpu.SMEM)] + [anywhere] * 5,
        out_specs=pl.BlockSpec(memory_space=pltpu.VMEM),
        scratch_shapes=[
            pltpu.VMEM((4, NB * BLK, FEAT), BF16),
            pltpu.VMEM((4, 3, FEAT, WIDTH), BF16),
            pltpu.VMEM((6, NB * BLK, 256), F32),
            pltpu.VMEM((2, NB, BLK, 256), BF16),
            pltpu.VMEM((2, 4, NB, BLK, PACK), BF16),
            pltpu.VMEM((2, 4, NB, BLK, PACK), BF16),
            pltpu.VMEM((2, 2 * NB, 6, HALF, UNIT), BF16),
            pltpu.VMEM((2, 2 * NB, 2, HALF, UNIT), BF16),
            pltpu.VMEM((2, 2, 2 * NB, BLK, UNIT), BF16),
            pltpu.VMEM((2, BLK, UNIT), BF16),
            pltpu.VMEM((4, 4, 4, 2, 16, FEAT), BF16),
            pltpu.VMEM((4, 2, NB * BLK, 256), BF16),
            pltpu.VMEM((3, 3, 8, 128), jnp.int32),
            pltpu.VMEM((3, 8, 128), jnp.int32),
            pltpu.VMEM((8, 128), jnp.int32),
            pltpu.SMEM((8, 128), jnp.int32),
            dma((7,)),
            dma((4, 3)),
            dma((2 * NB, 4)),
            dma((2 * NB, 4)),
            dma((3, 3)),
            dma((3, 3)),
            dma((2, NB + 2, 7)),
            dma((2, NB + 2, 7)),
            dma((2, 2 * NB, 6)),
            dma((2, 2 * NB, 6)),
            dma((16,)),
            dma((16,)),
            dma((2 * NB, 4)),
            dma((2 * NB, 4)),
        ],
        compiler_params=pltpu.CompilerParams(
            collective_id=0, has_side_effects=True, vmem_limit_bytes=58 * 2**20
        ),
    )(block_bucket, tokens, w_query, w_key, w_value, w_out)


def solution(mesh):
    placed = (
        P("seq", "head"),
        P(None, "head"),
        P(None, "head"),
        P(None, "head"),
        P("head", None),
        P("seq"),
    )
    return jax.shard_map(
        per_device, mesh=mesh, in_specs=placed, out_specs=P("seq", "head"), check_vma=False
    )
```

```python
import jax
import jax.numpy as jnp
from jax import lax
from jax.experimental import pallas as pl
from jax.experimental.pallas import tpu as pltpu
from jax.sharding import PartitionSpec as P

HDIM = 128
SCALE = HDIM ** (-0.5)
BLK = 128
HALF = BLK // 2
NB = 4
FEAT = 1024
WIDTH = 512
PACK = 512
UNIT = 256
MESH = pl.DeviceIdType.MESH
F32 = jnp.float32
BF16 = jnp.bfloat16


def wrap(n):
    return lax.rem(n + 4, 4)


def kernel(
    ids, tok, wq, wk, wv, wo, out,
    tk, w, acc, qs, s1a, s1b, tx, rel, fin, kvp, wov, mx,
    idg, idsend, part_v, part_s,
    loc_sem, wloc_sem, tok_s, tok_r, id_s, id_r, ag_s, ag_r, rs_s, rs_r, wo_s, wo_r, mx_s, mx_r,
):
    s = lax.axis_index("seq")
    y = lax.axis_index("head")
    x = s // 8
    z = lax.rem(s // 2, 4)
    c = lax.rem(s, 2)
    s1 = (s1a, s1b)
    px = lax.rem(x, 2) * 2 + x // 2
    wo6 = wo.reshape(4, 4, 2, 16, 4 * FEAT)
    started = []

    def place(px, pz, pc):
        return (px * 4 + pz) * 2 + pc

    def ring(axis, k):
        if axis == "y":
            return (s, wrap(y + k))
        if axis == "x":
            return (place(wrap(x + k), z, c), y)
        return (place(x, wrap(z + k), c), y)

    sibling = (place(x, z, 1 - c), y)
    peers = [sibling] + [ring(a, k) for a in ("y", "x", "z") for k in (1, 2, 3)]

    def remote(src, dst, send, recv, device):
        copy = pltpu.make_async_remote_copy(
            src_ref=src, dst_ref=dst, send_sem=send, recv_sem=recv,
            device_id=device, device_id_type=MESH,
        )
        copy.start()
        started.append(copy)
        return copy

    barrier = pltpu.get_barrier_semaphore()
    for peer in peers:
        pl.semaphore_signal(barrier, inc=1, device_id=peer, device_id_type=MESH)

    tok_local = pltpu.make_async_copy(tok, tk.at[0], loc_sem.at[0])
    tok_local.start()
    w_local = []
    for d in (0, 3, 1, 2):
        rows = pl.ds(pl.multiple_of(wrap(y + d) * FEAT, FEAT), FEAT)
        for j, ref in enumerate((wq, wk, wv)):
            copy = pltpu.make_async_copy(ref.at[rows, :], w.at[d, j], wloc_sem.at[d, j])
            copy.start()
            w_local.append(copy)
    mine = pl.ds(pl.multiple_of(y * FEAT, FEAT), FEAT)
    wo_local = []
    for h in range(4):
        src, dst = wo6.at[h, :, :, :, mine], wov.at[0, h % 2 * 2 + h // 2]
        wo_local.append(pltpu.make_async_copy(src, dst, loc_sem.at[3 + h]))
    for copy in wo_local:
        copy.start()

    pl.semaphore_wait(barrier, len(peers))

    wo_y = []
    row16 = pl.ds(pl.multiple_of(s * 16, 16), 16)
    for k in (1, 2, 3):
        cols = pl.ds(pl.multiple_of(wrap(y + k) * FEAT, FEAT), FEAT)
        wo_y.append(remote(wo.at[row16, cols], wov.at[4 - k, px, z, c], wo_s.at[k - 1], wo_r.at[k - 1], ring("y", k)))

    tok_c = {}
    tok_f = {}

    def send_tokens(k):
        rows = pl.ds(k * HALF, HALF)
        tok_c[k, 0] = remote(tok.at[rows, :], tk.at[3, rows, :], tok_s.at[k, 0], tok_r.at[k, 0], ring("y", 1))
        tok_c[k, 1] = remote(tok.at[rows, :], tk.at[1, rows, :], tok_s.at[k, 1], tok_r.at[k, 1], ring("y", -1))

    def tokens_event(k):
        lo, hi = pl.ds(k * HALF, HALF // 2), pl.ds(k * HALF + HALF // 2, HALF // 2)
        tok_c[k, 0].wait_recv()
        if k < 7:
            tok_f[k, 0] = remote(tk.at[3, lo, :], tk.at[2, lo, :], tok_s.at[k, 2], tok_r.at[k, 2], ring("y", 1))
        tok_c[k, 1].wait_recv()
        if k < 7:
            tok_f[k, 1] = remote(tk.at[1, hi, :], tk.at[2, hi, :], tok_s.at[k, 3], tok_r.at[k, 3], ring("y", -1))
        if k + 2 < 8:
            send_tokens(k + 2)
        if k == 6:
            rows = pl.ds(7 * HALF, HALF)
            tok_f[7, 0] = remote(tok.at[rows, :], tk.at[2, rows, :], tok_s.at[7, 2], tok_r.at[7, 2], ring("y", 2))

    send_tokens(0)
    send_tokens(1)

    lane = lax.broadcasted_iota(jnp.int32, (8, 128), 1)
    row = jnp.zeros((8, 128), jnp.int32)
    for i in range(NB):
        row = jnp.where(lane == s * NB + i, ids[i], row)

    def spread(stage, row, targets):
        idsend[stage] = row
        copies = []
        for k, target in targets:
            copies.append(
                remote(idsend.at[stage], idg.at[stage, k - 1], id_s.at[stage, k - 1], id_r.at[stage, k - 1], target)
            )
        return copies

    ids_x = spread(0, row, [(k, ring("x", k)) for k in (1, 2, 3)])

    tok_local.wait()
    for copy in w_local[:3]:
        copy.wait()

    def own_tile(t, carry):
        n, m = t // 2, lax.rem(t, 2)
        rows = pl.ds(pl.multiple_of(m * 256, 256), 256)
        cols = pl.ds(pl.multiple_of(lax.rem(n, 2) * 256, 256), 256)
        acc[n, rows, :] = jnp.dot(tk[0, rows, :], w[0, n // 2, :, cols], preferred_element_type=F32)
        return carry

    lax.fori_loop(0, 12, own_tile, 0)

    def near_tiles(i):
        rows = pl.ds(i * BLK, BLK)

        def tile(n, carry):
            cols = pl.ds(pl.multiple_of(lax.rem(n, 2) * 256, 256), 256)
            acc[n, rows, :] += jnp.dot(
                tk[3, rows, :], w[3, n // 2, :, cols], preferred_element_type=F32
            ) + jnp.dot(tk[1, rows, :], w[1, n // 2, :, cols], preferred_element_type=F32)
            return carry

        lax.fori_loop(0, 6, tile, 0)

    pieces = ((0, 0, BLK), (1, 0, BLK), (2, 0, HALF), (2, HALF, HALF), (3, 0, HALF), (3, HALF, HALF))

    def far_tiles(start, count, first, last):
        rows = pl.ds(start, count)

        def tile(n, carry):
            cols = pl.ds(pl.multiple_of(lax.rem(n, 2) * 256, 256), 256)
            acc[n, rows, :] += jnp.dot(tk[2, rows, :], w[2, n // 2, :, cols], preferred_element_type=F32)
            return carry

        lax.fori_loop(first, last, tile, 0)

    ag = {}
    axes = ("x", "z")

    def finish_keys(p):
        i, start, count = pieces[p]
        rows, part = pl.ds(i * BLK + start, count), pl.ds(start, count)
        first = (i * BLK + start) // HALF
        for k in range(first, first + count // HALF):
            tok_f[k, 0].wait_recv()
            if k < 7:
                tok_f[k, 1].wait_recv()
        far_tiles(i * BLK + start, count, 2, 6)
        for f in range(2):
            for j in range(2):
                head = pl.ds(j * HDIM, HDIM)
                s1[f][0, 0, i, part, pl.ds(j * 256, HDIM)] = acc[2 + f, rows, head].astype(BF16)
                s1[f][0, 0, i, part, pl.ds(j * 256 + HDIM, HDIM)] = acc[4 + f, rows, head].astype(BF16)
        for f in range(2):
            own, a = s1[f].at[0, 0, i, part], axes[f]
            for n, (k, d) in enumerate(((2, 2), (1, 3), (-1, 1))):
                ag[f, p, d] = remote(own, s1[f].at[0, d, i, part], ag_s.at[f, p, n], ag_r.at[f, p, n], ring(a, k))
            ag[f, p, "own"] = remote(own, s1[f].at[1, 0, i, part], ag_s.at[f, p, 3], ag_r.at[f, p, 3], sibling)

    def finish_query(i):
        rows = pl.ds(i * BLK, BLK)
        far_tiles(i * BLK, BLK, 0, 2)
        for f in range(2):
            qs[f, i] = acc[f, rows, :].astype(BF16)

    def to_sibling(p):
        i, start, count = pieces[p]
        part = pl.ds(start, count)
        for n, d in ((2, 2), (0, 3), (1, 1)):
            for f in range(2):
                ag[f, p, d].wait_recv()
                src, dst = s1[f].at[0, d, i, part], s1[f].at[1, d, i, part]
                ag[f, p, "s", d] = remote(src, dst, ag_s.at[f, p, 4 + n], ag_r.at[f, p, 4 + n], sibling)

    for copy in ids_x:
        copy.wait_recv()
    row = row + idg[0, 0] + idg[0, 1] + idg[0, 2]
    ids_z = spread(1, row, [(k, ring("z", k)) for k in (1, 2, 3)])

    for copy in wo_y:
        copy.wait_recv()
    left_cols, right_cols = pl.ds(0, 512), pl.ds(512, 512)
    three = pl.ds(1, 3)
    wo_1 = []
    for k in (2, 1, 3):
        own = wov.at[three, px, z, c, :, left_cols]
        wo_1.append(remote(own, own, wo_s.at[2 + k], wo_r.at[2 + k], ring("x", k)))
        own = wov.at[three, px, z, c, :, right_cols]
        wo_1.append(remote(own, own, wo_s.at[5 + k], wo_r.at[5 + k], ring("z", k)))

    tokens_event(0)
    for copy in w_local[3:]:
        copy.wait()
    for copy in ids_z:
        copy.wait_recv()
    row = row + idg[1, 0] + idg[1, 1] + idg[1, 2]
    ids_c = spread(2, row, [(1, sibling)])
    tokens_event(1)

    for copy in wo_1:
        copy.wait_recv()
    wo_2 = []
    for k in (2, 1, 3):
        own = wov.at[three, :, z, c, :, left_cols]
        wo_2.append(remote(own, own, wo_s.at[8 + k], wo_r.at[8 + k], ring("z", k)))
        own = wov.at[three, px, :, c, :, right_cols]
        wo_2.append(remote(own, own, wo_s.at[11 + k], wo_r.at[11 + k], ring("x", k)))

    near_tiles(0)
    ids_c[0].wait_recv()
    row = row + idg[2, 0]

    across = jnp.broadcast_to(row[0:1, :], (128, 128))
    down = across.T
    one = lax.broadcasted_iota(jnp.int32, (128, 128), 0)
    two = lax.broadcasted_iota(jnp.int32, (128, 128), 1)
    same = (across == down) & (one != two)
    partner = jnp.sum(jnp.where(same, one + 1, 0), axis=0, keepdims=True) - 1
    part_v[...] = jnp.broadcast_to(partner, (8, 128))
    part_copy = pltpu.make_async_copy(part_v, part_s, loc_sem.at[2])
    part_copy.start()

    tokens_event(2)
    finish_keys(0)
    tokens_event(3)
    finish_query(0)
    near_tiles(1)
    tokens_event(4)
    finish_keys(1)
    for copy in wo_2:
        copy.wait_recv()
    own = wov.at[three, :, :, c]
    wo_3 = remote(own, own, wo_s.at[15], wo_r.at[15], sibling)
    tokens_event(5)
    near_tiles(2)
    finish_keys(2)
    to_sibling(0)
    tokens_event(6)
    finish_query(1)
    finish_keys(3)
    tokens_event(7)
    near_tiles(3)
    finish_keys(4)
    finish_keys(5)
    to_sibling(1)
    to_sibling(2)
    finish_query(2)
    to_sibling(3)
    finish_query(3)
    part_copy.wait()
    to_sibling(4)
    to_sibling(5)

    def choice(f, k, i):
        dest = place(x, wrap(z + k), c) if f == 0 else place(wrap(x + k), z, c)
        p = part_s[0, dest * NB + i]
        at = jnp.maximum(p, 0)
        xp, zp = at // 32, lax.rem(at // 8, 4)
        cp, ip = lax.rem(at // 4, 2), lax.rem(at, 4)
        along, held = (xp - x, zp) if f == 0 else (zp - z, xp)
        return (lax.rem(cp + c, 2), wrap(along), ip), held, p

    second = ("z", "x")
    here = (z, x)
    for f in range(2):
        for p in range(len(pieces)):
            ag[f, p, "own"].wait_recv()
            for d in (1, 2, 3):
                ag[f, p, "s", d].wait_recv()

    low, high = pl.ds(0, HALF), pl.ds(HALF, HALF)
    rs = {}
    choices = {}

    def chosen(f, k, i):
        if (f, k, i) not in choices:
            choices[f, k, i] = choice(f, k, i)
        return choices[f, k, i]

    def pass_on(f, u, g, k, rows, to, dst, relay=None):
        i, j = divmod(u, 2)
        index, held, _ = chosen(f, k, i)
        packet = s1[f][index[0], index[1], index[2], rows, pl.ds(j * UNIT, UNIT)]
        if relay is not None:
            packet = jnp.where(held == here[f], packet, rel[f, u, relay])
        tx[f, u, g] = packet
        rs[f, u, g] = remote(tx.at[f, u, g], dst, rs_s.at[f, u, g], rs_r.at[f, u, g], ring(second[f], to))

    def relay_out(u):
        for f in range(2):
            pass_on(f, u, 0, 2, low, 1, rel.at[f, u, 0])
            pass_on(f, u, 1, 2, high, -1, rel.at[f, u, 1])

    def direct_out(u):
        for f in range(2):
            pass_on(f, u, 2, 1, high, 1, fin.at[f, 0, u, high])
            pass_on(f, u, 3, -1, low, -1, fin.at[f, 1, u, low])

    def merged_out(u):
        for f in range(2):
            rs[f, u, 0].wait_recv()
            pass_on(f, u, 4, 1, low, 1, fin.at[f, 0, u, low], 0)
            rs[f, u, 1].wait_recv()
            pass_on(f, u, 5, -1, high, -1, fin.at[f, 1, u, high], 1)

    mx_c = {}

    def send_mixed(u):
        i, j = divmod(u, 2)
        rows = pl.ds(i * BLK, BLK)
        own = mx.at[0, j, rows]
        if u == 7:
            mx_c[u, 2] = remote(own, mx.at[2, j, rows], mx_s.at[u, 2], mx_r.at[u, 2], ring("y", 2))
        mx_c[u, 0] = remote(own, mx.at[3, j, rows], mx_s.at[u, 0], mx_r.at[u, 0], ring("y", 1))
        mx_c[u, 1] = remote(own, mx.at[1, j, rows], mx_s.at[u, 1], mx_r.at[u, 1], ring("y", -1))

    def forward_mixed(u):
        i, j = divmod(u, 2)
        lo, hi = pl.ds(i * BLK, HALF), pl.ds(i * BLK + HALF, HALF)
        mx_c[u, 0].wait_recv()
        mx_c[u, 2] = remote(mx.at[3, j, lo], mx.at[2, j, lo], mx_s.at[u, 2], mx_r.at[u, 2], ring("y", 1))
        mx_c[u, 1].wait_recv()
        mx_c[u, 3] = remote(mx.at[1, j, hi], mx.at[2, j, hi], mx_s.at[u, 3], mx_r.at[u, 3], ring("y", -1))

    def attend(u):
        i, j = divmod(u, 2)
        rows = pl.ds(i * BLK, BLK)
        for f in range(2):
            for g in (2, 3, 4, 5):
                rs[f, u, g].wait_recv()
        kc, vc = pl.ds(j * UNIT, HDIM), pl.ds(j * UNIT + HDIM, HDIM)
        for f in range(2):
            index, held, p = chosen(f, 0, i)
            at_left, at_right = held == wrap(here[f] - 1), held == wrap(here[f] + 1)
            for half, from_left in ((low, jnp.logical_not(at_right)), (high, at_left)):
                packet = jnp.where(from_left, fin[f, 0, u, half], fin[f, 1, u, half])
                own = s1[f][index[0], index[1], index[2], half, pl.ds(j * UNIT, UNIT)]
                kvp[f, half] = jnp.where(held == here[f], own, packet)
            query = qs[f, i, :, pl.ds(j * HDIM, HDIM)]
            dims = (((1,), (1,)), ((), ()))
            near = lax.dot_general(query, s1[f][0, 0, i, :, kc], dims, preferred_element_type=F32) * SCALE
            far = lax.dot_general(query, kvp[f, :, :HDIM], dims, preferred_element_type=F32) * SCALE
            far = jnp.where(p >= 0, far, -1e30)
            top = jnp.maximum(jnp.max(near, axis=1, keepdims=True), jnp.max(far, axis=1, keepdims=True))
            near, far = jnp.exp(near - top), jnp.exp(far - top)
            total = jnp.sum(near, axis=1, keepdims=True) + jnp.sum(far, axis=1, keepdims=True)
            near, far = (near / total).astype(BF16), (far / total).astype(BF16)
            mixed = jnp.dot(near, s1[f][0, 0, i, :, vc], preferred_element_type=F32)
            mixed += jnp.dot(far, kvp[f, :, HDIM:], preferred_element_type=F32)
            mx[0, j, rows, pl.ds(f * HDIM, HDIM)] = mixed.astype(BF16)
        send_mixed(u)

    def project(start, count, steps, first=True, last=True):
        rows = pl.ds(start, count)

        def tile(n, carry):
            cols = pl.ds(pl.multiple_of(n * 256, 256), 256)
            total = jnp.zeros((count, 256), F32) if first else acc[n, rows, :]
            for d, j in steps:
                part = wov[d, pl.ds(2 * j, 2), :, :, :, cols].reshape(256, 256)
                total += jnp.dot(mx[d, j, rows, :], part, preferred_element_type=F32)
            if last:
                out[rows, cols] = total.astype(BF16)
            else:
                acc[n, rows, :] = total
            return carry

        lax.fori_loop(0, 4, tile, 0)

    def arrived(*units):
        for u in units:
            for n in (0, 1, 2) if u == 7 else (2, 3):
                mx_c[u, n].wait_recv()

    before_exchange = len(started)
    relay_out(0)
    relay_out(1)
    direct_out(0)
    direct_out(1)
    relay_out(2)
    for copy in started[:before_exchange]:
        copy.wait_send()
    merged_out(0)
    merged_out(1)
    direct_out(2)
    relay_out(3)
    direct_out(3)
    merged_out(2)
    relay_out(4)
    relay_out(5)
    attend(0)
    attend(1)
    merged_out(3)
    direct_out(4)
    relay_out(6)
    attend(2)
    merged_out(4)
    direct_out(5)
    relay_out(7)
    forward_mixed(0)
    merged_out(5)
    direct_out(6)
    attend(3)
    forward_mixed(1)
    merged_out(6)
    attend(4)
    direct_out(7)
    merged_out(7)
    forward_mixed(2)
    attend(5)
    forward_mixed(3)
    attend(6)
    attend(7)
    forward_mixed(4)
    forward_mixed(5)
    for copy in wo_local:
        copy.wait()
    wo_3.wait_recv()
    every = [(d, j) for d in range(4) for j in range(2)]
    arrived(0, 1, 2, 3)
    project(0, 256, every)
    forward_mixed(6)
    project(256, 256, [(0, 0), (0, 1), (3, 0), (1, 0)], True, False)
    for copy in rs.values():
        copy.wait_send()
    arrived(7)
    project(256, 256, [(3, 1), (1, 1)], False, False)
    arrived(4, 5)
    project(256, 128, [(2, 0), (2, 1)], False, True)
    arrived(6)
    project(384, 128, [(2, 0), (2, 1)], False, True)
    for copy in mx_c.values():
        copy.wait_send()


def per_device(tokens, w_query, w_key, w_value, w_out, block_bucket):
    anywhere = pl.BlockSpec(memory_space=pl.ANY)
    dma = pltpu.SemaphoreType.DMA
    return pl.pallas_call(
        kernel,
        out_shape=pltpu.VMEM((NB * BLK, FEAT), BF16),
        in_specs=[pl.BlockSpec(memory_space=pltpu.SMEM)] + [anywhere] * 5,
        out_specs=pl.BlockSpec(memory_space=pltpu.VMEM),
        scratch_shapes=[
            pltpu.VMEM((4, NB * BLK, FEAT), BF16),
            pltpu.VMEM((4, 3, FEAT, WIDTH), BF16),
            pltpu.VMEM((6, NB * BLK, 256), F32),
            pltpu.VMEM((2, NB, BLK, 256), BF16),
            pltpu.VMEM((2, 4, NB, BLK, PACK), BF16),
            pltpu.VMEM((2, 4, NB, BLK, PACK), BF16),
            pltpu.VMEM((2, 2 * NB, 6, HALF, UNIT), BF16),
            pltpu.VMEM((2, 2 * NB, 2, HALF, UNIT), BF16),
            pltpu.VMEM((2, 2, 2 * NB, BLK, UNIT), BF16),
            pltpu.VMEM((2, BLK, UNIT), BF16),
            pltpu.VMEM((4, 4, 4, 2, 16, FEAT), BF16),
            pltpu.VMEM((4, 2, NB * BLK, 256), BF16),
            pltpu.VMEM((3, 3, 8, 128), jnp.int32),
            pltpu.VMEM((3, 8, 128), jnp.int32),
            pltpu.VMEM((8, 128), jnp.int32),
            pltpu.SMEM((8, 128), jnp.int32),
            dma((7,)),
            dma((4, 3)),
            dma((2 * NB, 4)),
            dma((2 * NB, 4)),
            dma((3, 3)),
            dma((3, 3)),
            dma((2, NB + 2, 7)),
            dma((2, NB + 2, 7)),
            dma((2, 2 * NB, 6)),
            dma((2, 2 * NB, 6)),
            dma((16,)),
            dma((16,)),
            dma((2 * NB, 4)),
            dma((2 * NB, 4)),
        ],
        compiler_params=pltpu.CompilerParams(
            collective_id=0, has_side_effects=True, vmem_limit_bytes=58 * 2**20
        ),
    )(block_bucket, tokens, w_query, w_key, w_value, w_out)


def solution(mesh):
    placed = (
        P("seq", "head"),
        P(None, "head"),
        P(None, "head"),
        P(None, "head"),
        P("head", None),
        P("seq"),
    )
    return jax.shard_map(
        per_device, mesh=mesh, in_specs=placed, out_specs=P("seq", "head"), check_vma=False
    )
```

```python
import jax
import jax.numpy as jnp
from jax import lax
from jax.experimental import pallas as pl
from jax.experimental.pallas import tpu as pltpu
from jax.sharding import PartitionSpec as P

HDIM = 128
SCALE = HDIM ** (-0.5)
BLK = 128
HALF = BLK // 2
NB = 4
FEAT = 1024
WIDTH = 512
PACK = 512
UNIT = 256
MESH = pl.DeviceIdType.MESH
F32 = jnp.float32
BF16 = jnp.bfloat16


def wrap(n):
    return lax.rem(n + 4, 4)


def kernel(
    ids, tok, wq, wk, wv, wo, out,
    tk, w, acc, qs, s1a, s1b, tx, rel, fin, kvp, wov, mx,
    idg, idsend, part_v, part_s,
    loc_sem, wloc_sem, tok_s, tok_r, id_s, id_r, ag_s, ag_r, rs_s, rs_r, wo_s, wo_r, mx_s, mx_r,
):
    s = lax.axis_index("seq")
    y = lax.axis_index("head")
    x = s // 8
    z = lax.rem(s // 2, 4)
    c = lax.rem(s, 2)
    s1 = (s1a, s1b)
    px = lax.rem(x, 2) * 2 + x // 2
    wo6 = wo.reshape(4, 4, 2, 16, 4 * FEAT)
    started = []

    def place(px, pz, pc):
        return (px * 4 + pz) * 2 + pc

    def ring(axis, k):
        if axis == "y":
            return (s, wrap(y + k))
        if axis == "x":
            return (place(wrap(x + k), z, c), y)
        return (place(x, wrap(z + k), c), y)

    sibling = (place(x, z, 1 - c), y)
    peers = [sibling] + [ring(a, k) for a in ("y", "x", "z") for k in (1, 2, 3)]

    def remote(src, dst, send, recv, device):
        copy = pltpu.make_async_remote_copy(
            src_ref=src, dst_ref=dst, send_sem=send, recv_sem=recv,
            device_id=device, device_id_type=MESH,
        )
        copy.start()
        started.append(copy)
        return copy

    barrier = pltpu.get_barrier_semaphore()
    for peer in peers:
        pl.semaphore_signal(barrier, inc=1, device_id=peer, device_id_type=MESH)

    tok_local = pltpu.make_async_copy(tok, tk.at[0], loc_sem.at[0])
    tok_local.start()
    w_local = []
    for d in (0, 3, 1, 2):
        rows = pl.ds(pl.multiple_of(wrap(y + d) * FEAT, FEAT), FEAT)
        for j, ref in enumerate((wq, wk, wv)):
            copy = pltpu.make_async_copy(ref.at[rows, :], w.at[d, j], wloc_sem.at[d, j])
            copy.start()
            w_local.append(copy)
    mine = pl.ds(pl.multiple_of(y * FEAT, FEAT), FEAT)
    wo_local = []
    for h in range(4):
        src, dst = wo6.at[h, :, :, :, mine], wov.at[0, h % 2 * 2 + h // 2]
        wo_local.append(pltpu.make_async_copy(src, dst, loc_sem.at[3 + h]))
    for copy in wo_local:
        copy.start()

    pl.semaphore_wait(barrier, len(peers))

    wo_y = []
    row16 = pl.ds(pl.multiple_of(s * 16, 16), 16)
    for k in (1, 2, 3):
        cols = pl.ds(pl.multiple_of(wrap(y + k) * FEAT, FEAT), FEAT)
        wo_y.append(remote(wo.at[row16, cols], wov.at[4 - k, px, z, c], wo_s.at[k - 1], wo_r.at[k - 1], ring("y", k)))

    tok_c = {}
    tok_f = {}

    def send_tokens(k):
        rows = pl.ds(k * HALF, HALF)
        tok_c[k, 0] = remote(tok.at[rows, :], tk.at[3, rows, :], tok_s.at[k, 0], tok_r.at[k, 0], ring("y", 1))
        tok_c[k, 1] = remote(tok.at[rows, :], tk.at[1, rows, :], tok_s.at[k, 1], tok_r.at[k, 1], ring("y", -1))

    def tokens_event(k):
        lo, hi = pl.ds(k * HALF, HALF // 2), pl.ds(k * HALF + HALF // 2, HALF // 2)
        tok_c[k, 0].wait_recv()
        if k < 7:
            tok_f[k, 0] = remote(tk.at[3, lo, :], tk.at[2, lo, :], tok_s.at[k, 2], tok_r.at[k, 2], ring("y", 1))
        tok_c[k, 1].wait_recv()
        if k < 7:
            tok_f[k, 1] = remote(tk.at[1, hi, :], tk.at[2, hi, :], tok_s.at[k, 3], tok_r.at[k, 3], ring("y", -1))
        if k + 2 < 8:
            send_tokens(k + 2)
        if k == 6:
            rows = pl.ds(7 * HALF, HALF)
            tok_f[7, 0] = remote(tok.at[rows, :], tk.at[2, rows, :], tok_s.at[7, 2], tok_r.at[7, 2], ring("y", 2))

    send_tokens(0)
    send_tokens(1)

    lane = lax.broadcasted_iota(jnp.int32, (8, 128), 1)
    row = jnp.zeros((8, 128), jnp.int32)
    for i in range(NB):
        row = jnp.where(lane == s * NB + i, ids[i], row)

    def spread(stage, row, targets):
        idsend[stage] = row
        copies = []
        for k, target in targets:
            copies.append(
                remote(idsend.at[stage], idg.at[stage, k - 1], id_s.at[stage, k - 1], id_r.at[stage, k - 1], target)
            )
        return copies

    ids_x = spread(0, row, [(k, ring("x", k)) for k in (1, 2, 3)])

    tok_local.wait()
    for copy in w_local[:3]:
        copy.wait()

    def own_tile(t, carry):
        n, m = t // 2, lax.rem(t, 2)
        rows = pl.ds(pl.multiple_of(m * 256, 256), 256)
        cols = pl.ds(pl.multiple_of(lax.rem(n, 2) * 256, 256), 256)
        acc[n, rows, :] = jnp.dot(tk[0, rows, :], w[0, n // 2, :, cols], preferred_element_type=F32)
        return carry

    lax.fori_loop(0, 12, own_tile, 0)

    def near_tiles(i):
        rows = pl.ds(i * BLK, BLK)

        def tile(n, carry):
            cols = pl.ds(pl.multiple_of(lax.rem(n, 2) * 256, 256), 256)
            acc[n, rows, :] += jnp.dot(
                tk[3, rows, :], w[3, n // 2, :, cols], preferred_element_type=F32
            ) + jnp.dot(tk[1, rows, :], w[1, n // 2, :, cols], preferred_element_type=F32)
            return carry

        lax.fori_loop(0, 6, tile, 0)

    pieces = ((0, 0, BLK), (1, 0, BLK), (2, 0, HALF), (2, HALF, HALF), (3, 0, HALF), (3, HALF, HALF))

    def far_tiles(start, count, first, last):
        rows = pl.ds(start, count)

        def tile(n, carry):
            cols = pl.ds(pl.multiple_of(lax.rem(n, 2) * 256, 256), 256)
            acc[n, rows, :] += jnp.dot(tk[2, rows, :], w[2, n // 2, :, cols], preferred_element_type=F32)
            return carry

        lax.fori_loop(first, last, tile, 0)

    ag = {}
    axes = ("x", "z")

    def finish_keys(p):
        i, start, count = pieces[p]
        rows, part = pl.ds(i * BLK + start, count), pl.ds(start, count)
        first = (i * BLK + start) // HALF
        for k in range(first, first + count // HALF):
            tok_f[k, 0].wait_recv()
            if k < 7:
                tok_f[k, 1].wait_recv()
        far_tiles(i * BLK + start, count, 2, 6)
        for f in range(2):
            for j in range(2):
                head = pl.ds(j * HDIM, HDIM)
                s1[f][0, 0, i, part, pl.ds(j * 256, HDIM)] = acc[2 + f, rows, head].astype(BF16)
                s1[f][0, 0, i, part, pl.ds(j * 256 + HDIM, HDIM)] = acc[4 + f, rows, head].astype(BF16)
        for f in range(2):
            own, a = s1[f].at[0, 0, i, part], axes[f]
            for n, (k, d) in enumerate(((2, 2), (1, 3), (-1, 1))):
                ag[f, p, d] = remote(own, s1[f].at[0, d, i, part], ag_s.at[f, p, n], ag_r.at[f, p, n], ring(a, k))
            ag[f, p, "own"] = remote(own, s1[f].at[1, 0, i, part], ag_s.at[f, p, 3], ag_r.at[f, p, 3], sibling)

    def finish_query(i):
        rows = pl.ds(i * BLK, BLK)
        far_tiles(i * BLK, BLK, 0, 2)
        for f in range(2):
            qs[f, i] = acc[f, rows, :].astype(BF16)

    def to_sibling(p):
        i, start, count = pieces[p]
        part = pl.ds(start, count)
        for n, d in ((2, 2), (0, 3), (1, 1)):
            for f in range(2):
                ag[f, p, d].wait_recv()
                src, dst = s1[f].at[0, d, i, part], s1[f].at[1, d, i, part]
                ag[f, p, "s", d] = remote(src, dst, ag_s.at[f, p, 4 + n], ag_r.at[f, p, 4 + n], sibling)

    for copy in ids_x:
        copy.wait_recv()
    row = row + idg[0, 0] + idg[0, 1] + idg[0, 2]
    ids_z = spread(1, row, [(k, ring("z", k)) for k in (1, 2, 3)])

    for copy in wo_y:
        copy.wait_recv()
    left_cols, right_cols = pl.ds(0, 512), pl.ds(512, 512)
    three = pl.ds(1, 3)
    wo_1 = []
    for k in (2, 1, 3):
        own = wov.at[three, px, z, c, :, left_cols]
        wo_1.append(remote(own, own, wo_s.at[2 + k], wo_r.at[2 + k], ring("x", k)))
        own = wov.at[three, px, z, c, :, right_cols]
        wo_1.append(remote(own, own, wo_s.at[5 + k], wo_r.at[5 + k], ring("z", k)))

    tokens_event(0)
    for copy in w_local[3:]:
        copy.wait()
    for copy in ids_z:
        copy.wait_recv()
    row = row + idg[1, 0] + idg[1, 1] + idg[1, 2]
    ids_c = spread(2, row, [(1, sibling)])
    tokens_event(1)

    for copy in wo_1:
        copy.wait_recv()
    wo_2 = []
    for k in (2, 1, 3):
        own = wov.at[three, :, z, c, :, left_cols]
        wo_2.append(remote(own, own, wo_s.at[8 + k], wo_r.at[8 + k], ring("z", k)))
        own = wov.at[three, px, :, c, :, right_cols]
        wo_2.append(remote(own, own, wo_s.at[11 + k], wo_r.at[11 + k], ring("x", k)))

    near_tiles(0)
    ids_c[0].wait_recv()
    row = row + idg[2, 0]

    across = jnp.broadcast_to(row[0:1, :], (128, 128))
    down = across.T
    one = lax.broadcasted_iota(jnp.int32, (128, 128), 0)
    two = lax.broadcasted_iota(jnp.int32, (128, 128), 1)
    same = (across == down) & (one != two)
    partner = jnp.sum(jnp.where(same, one + 1, 0), axis=0, keepdims=True) - 1
    part_v[...] = jnp.broadcast_to(partner, (8, 128))
    part_copy = pltpu.make_async_copy(part_v, part_s, loc_sem.at[2])
    part_copy.start()

    tokens_event(2)
    finish_keys(0)
    tokens_event(3)
    finish_query(0)
    near_tiles(1)
    tokens_event(4)
    finish_keys(1)
    for copy in wo_2:
        copy.wait_recv()
    own = wov.at[three, :, :, c]
    wo_3 = remote(own, own, wo_s.at[15], wo_r.at[15], sibling)
    tokens_event(5)
    near_tiles(2)
    finish_keys(2)
    to_sibling(0)
    tokens_event(6)
    finish_query(1)
    finish_keys(3)
    tokens_event(7)
    near_tiles(3)
    finish_keys(4)
    finish_keys(5)
    to_sibling(1)
    to_sibling(2)
    finish_query(2)
    to_sibling(3)
    finish_query(3)
    part_copy.wait()
    to_sibling(4)
    to_sibling(5)

    def choice(f, k, i):
        dest = place(x, wrap(z + k), c) if f == 0 else place(wrap(x + k), z, c)
        p = part_s[0, dest * NB + i]
        at = jnp.maximum(p, 0)
        xp, zp = at // 32, lax.rem(at // 8, 4)
        cp, ip = lax.rem(at // 4, 2), lax.rem(at, 4)
        along, held = (xp - x, zp) if f == 0 else (zp - z, xp)
        return (lax.rem(cp + c, 2), wrap(along), ip), held, p

    second = ("z", "x")
    here = (z, x)
    for f in range(2):
        for p in range(len(pieces)):
            ag[f, p, "own"].wait_recv()
            for d in (1, 2, 3):
                ag[f, p, "s", d].wait_recv()

    low, high = pl.ds(0, HALF), pl.ds(HALF, HALF)
    rs = {}
    choices = {}

    def chosen(f, k, i):
        if (f, k, i) not in choices:
            choices[f, k, i] = choice(f, k, i)
        return choices[f, k, i]

    def pass_on(f, u, g, k, rows, to, dst, relay=None):
        i, j = divmod(u, 2)
        index, held, _ = chosen(f, k, i)
        packet = s1[f][index[0], index[1], index[2], rows, pl.ds(j * UNIT, UNIT)]
        if relay is not None:
            packet = jnp.where(held == here[f], packet, rel[f, u, relay])
        tx[f, u, g] = packet
        rs[f, u, g] = remote(tx.at[f, u, g], dst, rs_s.at[f, u, g], rs_r.at[f, u, g], ring(second[f], to))

    def relay_out(u):
        for f in range(2):
            pass_on(f, u, 0, 2, low, 1, rel.at[f, u, 0])
            pass_on(f, u, 1, 2, high, -1, rel.at[f, u, 1])

    def direct_out(u):
        for f in range(2):
            pass_on(f, u, 2, 1, high, 1, fin.at[f, 0, u, high])
            pass_on(f, u, 3, -1, low, -1, fin.at[f, 1, u, low])

    def merged_out(u):
        for f in range(2):
            rs[f, u, 0].wait_recv()
            pass_on(f, u, 4, 1, low, 1, fin.at[f, 0, u, low], 0)
            rs[f, u, 1].wait_recv()
            pass_on(f, u, 5, -1, high, -1, fin.at[f, 1, u, high], 1)

    mx_c = {}

    def send_mixed(u):
        i, j = divmod(u, 2)
        rows = pl.ds(i * BLK, BLK)
        own = mx.at[0, j, rows]
        if u == 7:
            mx_c[u, 2] = remote(own, mx.at[2, j, rows], mx_s.at[u, 2], mx_r.at[u, 2], ring("y", 2))
        mx_c[u, 0] = remote(own, mx.at[3, j, rows], mx_s.at[u, 0], mx_r.at[u, 0], ring("y", 1))
        mx_c[u, 1] = remote(own, mx.at[1, j, rows], mx_s.at[u, 1], mx_r.at[u, 1], ring("y", -1))

    def forward_mixed(u):
        i, j = divmod(u, 2)
        lo, hi = pl.ds(i * BLK, HALF), pl.ds(i * BLK + HALF, HALF)
        mx_c[u, 0].wait_recv()
        mx_c[u, 2] = remote(mx.at[3, j, lo], mx.at[2, j, lo], mx_s.at[u, 2], mx_r.at[u, 2], ring("y", 1))
        mx_c[u, 1].wait_recv()
        mx_c[u, 3] = remote(mx.at[1, j, hi], mx.at[2, j, hi], mx_s.at[u, 3], mx_r.at[u, 3], ring("y", -1))

    def attend(u):
        i, j = divmod(u, 2)
        rows = pl.ds(i * BLK, BLK)
        for f in range(2):
            for g in (2, 3, 4, 5):
                rs[f, u, g].wait_recv()
        kc, vc = pl.ds(j * UNIT, HDIM), pl.ds(j * UNIT + HDIM, HDIM)
        for f in range(2):
            index, held, p = chosen(f, 0, i)
            at_left, at_right = held == wrap(here[f] - 1), held == wrap(here[f] + 1)
            for half, from_left in ((low, jnp.logical_not(at_right)), (high, at_left)):
                packet = jnp.where(from_left, fin[f, 0, u, half], fin[f, 1, u, half])
                own = s1[f][index[0], index[1], index[2], half, pl.ds(j * UNIT, UNIT)]
                kvp[f, half] = jnp.where(held == here[f], own, packet)
            query = qs[f, i, :, pl.ds(j * HDIM, HDIM)]
            dims = (((1,), (1,)), ((), ()))
            near = lax.dot_general(query, s1[f][0, 0, i, :, kc], dims, preferred_element_type=F32) * SCALE
            far = lax.dot_general(query, kvp[f, :, :HDIM], dims, preferred_element_type=F32) * SCALE
            far = jnp.where(p >= 0, far, -1e30)
            top = jnp.maximum(jnp.max(near, axis=1, keepdims=True), jnp.max(far, axis=1, keepdims=True))
            near, far = jnp.exp(near - top), jnp.exp(far - top)
            total = jnp.sum(near, axis=1, keepdims=True) + jnp.sum(far, axis=1, keepdims=True)
            near, far = (near / total).astype(BF16), (far / total).astype(BF16)
            mixed = jnp.dot(near, s1[f][0, 0, i, :, vc], preferred_element_type=F32)
            mixed += jnp.dot(far, kvp[f, :, HDIM:], preferred_element_type=F32)
            mx[0, j, rows, pl.ds(f * HDIM, HDIM)] = mixed.astype(BF16)
        send_mixed(u)

    def project(start, count, steps, first=True, last=True):
        rows = pl.ds(start, count)

        def tile(n, carry):
            cols = pl.ds(pl.multiple_of(n * 256, 256), 256)
            total = jnp.zeros((count, 256), F32) if first else acc[n, rows, :]
            for d, j in steps:
                part = wov[d, pl.ds(2 * j, 2), :, :, :, cols].reshape(256, 256)
                total += jnp.dot(mx[d, j, rows, :], part, preferred_element_type=F32)
            if last:
                out[rows, cols] = total.astype(BF16)
            else:
                acc[n, rows, :] = total
            return carry

        lax.fori_loop(0, 4, tile, 0)

    def arrived(*units):
        for u in units:
            for n in (0, 1, 2) if u == 7 else (2, 3):
                mx_c[u, n].wait_recv()

    before_exchange = len(started)
    relay_out(0)
    relay_out(1)
    direct_out(0)
    direct_out(1)
    relay_out(2)
    for copy in started[:before_exchange]:
        copy.wait_send()
    merged_out(0)
    merged_out(1)
    direct_out(2)
    relay_out(3)
    direct_out(3)
    merged_out(2)
    relay_out(4)
    attend(0)
    relay_out(5)
    attend(1)
    merged_out(3)
    direct_out(4)
    relay_out(6)
    attend(2)
    merged_out(4)
    direct_out(5)
    relay_out(7)
    forward_mixed(0)
    merged_out(5)
    direct_out(6)
    attend(3)
    forward_mixed(1)
    merged_out(6)
    attend(4)
    direct_out(7)
    merged_out(7)
    forward_mixed(2)
    attend(5)
    forward_mixed(3)
    attend(6)
    attend(7)
    forward_mixed(4)
    forward_mixed(5)
    for copy in wo_local:
        copy.wait()
    wo_3.wait_recv()
    every = [(d, j) for d in range(4) for j in range(2)]
    arrived(0, 1, 2, 3)
    project(0, 256, every)
    forward_mixed(6)
    project(256, 256, [(0, 0), (0, 1), (3, 0), (1, 0)], True, False)
    for copy in rs.values():
        copy.wait_send()
    arrived(7)
    project(256, 256, [(3, 1), (1, 1)], False, False)
    arrived(4, 5)
    project(256, 128, [(2, 0), (2, 1)], False, True)
    arrived(6)
    project(384, 128, [(2, 0), (2, 1)], False, True)
    for copy in mx_c.values():
        copy.wait_send()


def per_device(tokens, w_query, w_key, w_value, w_out, block_bucket):
    anywhere = pl.BlockSpec(memory_space=pl.ANY)
    dma = pltpu.SemaphoreType.DMA
    return pl.pallas_call(
        kernel,
        out_shape=pltpu.VMEM((NB * BLK, FEAT), BF16),
        in_specs=[pl.BlockSpec(memory_space=pltpu.SMEM)] + [anywhere] * 5,
        out_specs=pl.BlockSpec(memory_space=pltpu.VMEM),
        scratch_shapes=[
            pltpu.VMEM((4, NB * BLK, FEAT), BF16),
            pltpu.VMEM((4, 3, FEAT, WIDTH), BF16),
            pltpu.VMEM((6, NB * BLK, 256), F32),
            pltpu.VMEM((2, NB, BLK, 256), BF16),
            pltpu.VMEM((2, 4, NB, BLK, PACK), BF16),
            pltpu.VMEM((2, 4, NB, BLK, PACK), BF16),
            pltpu.VMEM((2, 2 * NB, 6, HALF, UNIT), BF16),
            pltpu.VMEM((2, 2 * NB, 2, HALF, UNIT), BF16),
            pltpu.VMEM((2, 2, 2 * NB, BLK, UNIT), BF16),
            pltpu.VMEM((2, BLK, UNIT), BF16),
            pltpu.VMEM((4, 4, 4, 2, 16, FEAT), BF16),
            pltpu.VMEM((4, 2, NB * BLK, 256), BF16),
            pltpu.VMEM((3, 3, 8, 128), jnp.int32),
            pltpu.VMEM((3, 8, 128), jnp.int32),
            pltpu.VMEM((8, 128), jnp.int32),
            pltpu.SMEM((8, 128), jnp.int32),
            dma((7,)),
            dma((4, 3)),
            dma((2 * NB, 4)),
            dma((2 * NB, 4)),
            dma((3, 3)),
            dma((3, 3)),
            dma((2, NB + 2, 7)),
            dma((2, NB + 2, 7)),
            dma((2, 2 * NB, 6)),
            dma((2, 2 * NB, 6)),
            dma((16,)),
            dma((16,)),
            dma((2 * NB, 4)),
            dma((2 * NB, 4)),
        ],
        compiler_params=pltpu.CompilerParams(
            collective_id=0, has_side_effects=True, vmem_limit_bytes=58 * 2**20
        ),
    )(block_bucket, tokens, w_query, w_key, w_value, w_out)


def solution(mesh):
    placed = (
        P("seq", "head"),
        P(None, "head"),
        P(None, "head"),
        P(None, "head"),
        P("head", None),
        P("seq"),
    )
    return jax.shard_map(
        per_device, mesh=mesh, in_specs=placed, out_specs=P("seq", "head"), check_vma=False
    )
```
